256 devices in a mesh: ty: 8 (over x, core), tx: 8 (over z), scan: 4 (over y).
Axes of the slice: x: 4, y: 4, z: 8, core: 2. Of those that a mesh axis runs over, the one named last changes fastest.
Arguments:
- specimen: float32 [2, 2, 2048, 2048], P(None, None, 'ty', 'tx'), may hold values from -1 to 1
- probe_modes: float32 [4, 2, 128, 128], replicated, may hold values from -3 to 3
- kernel_phase: float32 [128, 128], replicated, may hold values from -3.140625 to 3.140625
- offsets: int32 [8, 8, 8, 2], P('ty', 'tx', 'scan'), may hold values from -64 to 191, as said below
- live_counts: int32 [8, 8, 4], P('ty', 'tx', 'scan'), may hold values from 1 to 2, as said below
- measured: float32 [8, 8, 8, 128, 128], P('ty', 'tx', 'scan'), may hold values from 0 to 2
Outputs:
- object_grad: float32 [2, 2, 2048, 2048], P(None, None, 'ty', 'tx')
- probe_grad: float32 [4, 2, 128, 128], replicated
The draws below stay inside these ranges and needn't reach their ends.
Inputs may be any that keep to these rules, and one draw needn't show every extreme that they name: `offsets`: every patch lies inside the object; a patch's top-left lies between -64 and 191 relative to its tile, so it reaches at most 64 pixels into neighbouring tiles. Slots at or beyond a device's live count carry positions too but add nothing. `live_counts`: number of live slots of each device; the live slots are the first ones.
All inputs are finite; a program needn't handle non-finite values.
Results may differ from the reference program's by a relative error of at most 0.00022.
Values sent between devices are 32-bit elements; how exact they have to be, the bound alone decides.
No kernel may reach another device: no remote copies, remote signals or barrier semaphores. Data moves between devices by JAX's collectives and lax.ppermute only.
A program may use at most 64 MiB of HBM per device.

```python
import jax
import jax.numpy as jnp
from jax import lax

W = 128
MODES = 4
SLICES = 2
TILE = 256
SLOTS = 2
HALF = 64
GY = 8
GX = 8
NSC = 4
SLOTS_ALL = 8
NY = 2048
NX = 2048


def draw_offsets(key, part):
    key = jax.random.fold_in(key, 11)
    keys = jax.random.split(key, 10)
    shape = (GY, GX, SLOTS_ALL)
    tile_row = jnp.broadcast_to(jnp.arange(GY, dtype=jnp.int32)[:, None, None], shape)
    tile_col = jnp.broadcast_to(jnp.arange(GX, dtype=jnp.int32)[None, :, None], shape)
    slot = jnp.broadcast_to(jnp.arange(SLOTS_ALL, dtype=jnp.int32)[None, None, :], shape)
    row_low = jnp.where(tile_row == 0, 0, -HALF)
    row_high = jnp.where(tile_row == GY - 1, TILE - W, TILE - HALF - 1)
    col_low = jnp.where(tile_col == 0, 0, -HALF)
    col_high = jnp.where(tile_col == GX - 1, TILE - W, TILE - HALF - 1)
    rows = jax.random.randint(keys[0], shape, row_low, row_high + 1)
    cols = jax.random.randint(keys[1], shape, col_low, col_high + 1)
    pick_a = jax.random.randint(keys[2], (), 0, GX)
    slot_a = jax.random.randint(keys[3], (), 0, SLOTS_ALL)
    rows = jnp.where((tile_row == 0) & (tile_col == pick_a) & (slot == slot_a), TILE - HALF - 1, rows)
    pick_b = jax.random.randint(keys[4], (), 0, GX)
    slot_b = jax.random.randint(keys[5], (), 0, SLOTS_ALL)
    rows = jnp.where((tile_row == GY - 1) & (tile_col == pick_b) & (slot == slot_b), -HALF, rows)
    pick_c = jax.random.randint(keys[6], (), 0, GY)
    slot_c = jax.random.randint(keys[7], (), 0, SLOTS_ALL)
    cols = jnp.where((tile_col == 0) & (tile_row == pick_c) & (slot == slot_c), TILE - HALF - 1, cols)
    pick_d = jax.random.randint(keys[8], (), 0, GY)
    slot_d = jax.random.randint(keys[9], (), 0, SLOTS_ALL)
    cols = jnp.where((tile_col == GX - 1) & (tile_row == pick_d) & (slot == slot_d), -HALF, cols)
    return jnp.stack([rows, cols], axis=-1).astype(jnp.int32)


def draw_live_counts(key, part):
    key = jax.random.fold_in(key, 12)
    keys = jax.random.split(key, 3)
    shape = (GY, GX, NSC)
    tile_row = jnp.broadcast_to(jnp.arange(GY, dtype=jnp.int32)[:, None, None], shape)
    tile_col = jnp.broadcast_to(jnp.arange(GX, dtype=jnp.int32)[None, :, None], shape)
    counts = jax.random.randint(keys[0], shape, 1, SLOTS + 1)
    border = (tile_row == 0) | (tile_row == GY - 1) | (tile_col == 0) | (tile_col == GX - 1)
    counts = jnp.where(border, (counts + 1) // 2, counts)
    total = GY * GX * NSC
    flat = jnp.arange(total, dtype=jnp.int32).reshape(shape)
    first = jax.random.randint(keys[1], (), 0, total)
    second = (first + 1 + jax.random.randint(keys[2], (), 0, total - 1)) % total
    counts = jnp.where(flat == first, SLOTS, counts)
    counts = jnp.where(flat == second, 1, counts)
    return counts.astype(jnp.int32)


def levels(stream_key, extent, pieces, smallest, high):
    level, own = 1.0, jax.random.fold_in(stream_key, 6)
    for axis_at, parts in pieces:
        steps = jnp.exp(jax.random.uniform(jax.random.fold_in(own, axis_at), (parts,), jnp.float32, smallest / len(pieces), high / len(pieces)))
        level = level * jnp.repeat(steps, extent[axis_at] // parts).reshape([-1 if axis == axis_at else 1 for axis in range(len(extent))])
    return level


def gaussian(stream_key, dims, width, reach, held_as=jnp.bfloat16):
    entries = jax.random.normal(stream_key, dims, jnp.float32) * width
    return jnp.minimum(jnp.maximum(entries, -reach), reach).astype(held_as)


def setup_inputs(seed: int = 0) -> dict:
    arg_keys = jax.random.split(jax.random.key(seed), 7)
    specimen = jnp.clip(jax.random.uniform(arg_keys[0], (SLICES, 2, NY, NX), jnp.float32, -1.0, 1.0) * levels(arg_keys[0], (SLICES, 2, NY, NX), ((2, 8), (3, 8)), -0.4, 0.0), -1.0, 1.0)
    probe_modes = gaussian(arg_keys[1], (MODES, 2, W, W), 0.5, 3.0, jnp.float32)
    kernel_phase = jnp.clip(jax.random.uniform(arg_keys[2], (W, W), jnp.float32, -3.140625, 3.140625), -3.140625, 3.140625)
    offsets = draw_offsets(jax.random.fold_in(arg_keys[6], 71), 0)
    live_counts = draw_live_counts(jax.random.fold_in(arg_keys[6], 71), 0)
    measured = jnp.clip(2.0 * jax.random.uniform(arg_keys[5], (GY, GX, SLOTS_ALL, W, W), jnp.float32) ** levels(arg_keys[5], (GY, GX, SLOTS_ALL, W, W), ((0, 8), (1, 8), (2, 4)), -0.2, 0.2), 0.0, 2.0)
    return {"specimen": specimen, "probe_modes": probe_modes, "kernel_phase": kernel_phase, "offsets": offsets, "live_counts": live_counts, "measured": measured}


def slot_loss(object_patch, probe_modes, kernel_phase, recorded, weight_live):
    layers = lax.complex(object_patch[:, 0], object_patch[:, 1])
    wavefield = lax.complex(probe_modes[:, 0], probe_modes[:, 1])
    kernel = lax.complex(jnp.cos(kernel_phase), jnp.sin(kernel_phase))
    for layer in range(SLICES):
        wavefield = wavefield * layers[layer]
        if layer + 1 < SLICES:
            spectrum = jnp.fft.fft2(wavefield, axes=(-2, -1), norm='ortho') * kernel
            wavefield = jnp.fft.ifft2(spectrum, axes=(-2, -1), norm='ortho')
    farfield = jnp.fft.fft2(wavefield, axes=(-2, -1), norm='ortho')
    intensity = lax.optimization_barrier(jnp.sum(farfield.real * farfield.real + farfield.imag * farfield.imag, axis=0))
    return 0.5 * weight_live * jnp.sum((intensity - recorded) ** 2)

def reference(specimen, probe_modes, kernel_phase, offsets, live_counts, measured):
    total = GY * GX * SLOTS_ALL
    indices = jnp.arange(total, dtype=jnp.int32)
    tile_row = indices // (GX * SLOTS_ALL)
    tile_col = indices // SLOTS_ALL % GX
    slot = indices % SLOTS_ALL
    group = slot // SLOTS
    within = slot % SLOTS
    corners = offsets.reshape(total, 2)
    row_start = (tile_row * TILE + corners[:, 0]).astype(jnp.int32)
    col_start = (tile_col * TILE + corners[:, 1]).astype(jnp.int32)
    limits = live_counts.reshape(-1)[(tile_row * GX + tile_col) * NSC + group]
    weights = (within < limits).astype(jnp.float32)
    patterns = measured.reshape(total, W, W)
    gradient_fn = jax.grad(slot_loss, argnums=(0, 1))
    anchor = jnp.zeros((), jnp.int32)

    def visit(carried, inputs):
        object_total, probe_total = carried
        row_at, col_at, recorded, weight_live = inputs
        object_patch = lax.dynamic_slice(specimen, (anchor, anchor, row_at, col_at), (SLICES, 2, W, W))
        patch_grad, probe_part = gradient_fn(object_patch, probe_modes, kernel_phase, recorded, weight_live)
        current = lax.dynamic_slice(object_total, (anchor, anchor, row_at, col_at), (SLICES, 2, W, W))
        object_total = lax.dynamic_update_slice(object_total, current + patch_grad, (anchor, anchor, row_at, col_at))
        return ((object_total, probe_total + probe_part), None)
    start = (jnp.zeros(specimen.shape, jnp.float32), jnp.zeros(probe_modes.shape, jnp.float32))
    (object_grad, probe_total), _ = lax.scan(visit, start, (row_start, col_start, patterns, weights))
    live_total = jnp.sum(live_counts).astype(jnp.float32)
    return (object_grad, probe_total / live_total)
```

```python
import functools

import jax
import jax.numpy as jnp
import numpy as np
from jax import lax
from jax.experimental import pallas as pl
from jax.experimental.pallas import tpu as pltpu
from jax.sharding import Mesh
from jax.sharding import PartitionSpec as P

F32 = jnp.float32
BF16 = jnp.bfloat16
VMEM = pl.BlockSpec(memory_space=pltpu.VMEM)
SMEM = pl.BlockSpec(memory_space=pltpu.SMEM)
PARAMS = pltpu.CompilerParams(vmem_limit_bytes=48 * 1024 * 1024)
W = 128
HALF = 64
TILE = 256
MODES = 4


def call(body, outs, args, specs, scratch=(), name=None):
    return pl.pallas_call(
        body,
        out_shape=[jax.ShapeDtypeStruct(shape, F32) for shape in outs],
        in_specs=specs,
        out_specs=[VMEM] * len(outs),
        scratch_shapes=list(scratch),
        compiler_params=PARAMS,
        name=name,
    )(*args)


def low_lanes(rows):
    return lax.broadcasted_iota(jnp.int32, (rows, W), 1) < HALF


def swap(x):
    return pltpu.roll(x, HALF, 1)


def pack_body(meta, tile, to_left, to_right, to_core, to_far, core_left, core_right, far_left, far_right):
    core = meta[0]
    core_row = pl.multiple_of((1 - core) * (TILE - HALF), HALF)
    far_row = pl.multiple_of(core * (TILE - HALF), HALF)
    wide = low_lanes(W)
    short = low_lanes(HALF // 2)
    for part in range(4):
        first, second = tile[part, :W, :W], tile[part, W:, :W]
        to_left[part] = jnp.where(wide, first, swap(second))
        first, second = tile[part, :W, W:], tile[part, W:, W:]
        to_right[part] = jnp.where(wide, swap(first), second)
        for row, strip, left, right in (
            (core_row, to_core, core_left, core_right),
            (far_row, to_far, far_left, far_right),
        ):
            rows = tile[part, pl.ds(row, HALF), :]
            strip[part] = rows
            upper, lower = rows[: HALF // 2], rows[HALF // 2 :]
            left[part] = jnp.where(short, upper[:, :W], swap(lower[:, :W]))
            right[part] = jnp.where(short, swap(upper[:, W:]), lower[:, W:])


def halves(x):
    high = x.astype(BF16)
    return high, (x - high.astype(F32)).astype(BF16)


def times_right(real, imag, table):
    high, low = halves(
        jnp.concatenate([jnp.concatenate([r, i], axis=1) for r, i in zip(real, imag)], axis=0)
    )
    out = jnp.dot(jnp.concatenate([high, low, high], axis=1), table, preferred_element_type=F32)
    blocks = [out[W * m : W * (m + 1)] for m in range(len(real))]
    return [b[:, :W] for b in blocks], [b[:, W:] for b in blocks]


def times_left(table, real, imag):
    high, low = halves(
        jnp.concatenate([jnp.concatenate(real, axis=1), jnp.concatenate(imag, axis=1)], axis=0)
    )
    out = jnp.dot(table, jnp.concatenate([high, low, high], axis=0), preferred_element_type=F32)
    cols = [out[:, W * m : W * (m + 1)] for m in range(len(real))]
    return [c[:W] for c in cols], [c[W:] for c in cols]


def slots_body(
    meta,
    tile,
    from_right,
    from_left,
    from_core,
    from_far,
    core_right,
    core_left,
    far_right,
    far_left,
    probe,
    kernel_real,
    kernel_imag,
    measured,
    right_high,
    right_low,
    left_high,
    left_low,
    out0,
    out1,
    out2,
    out3,
    probe_send,
    probe_keep,
    wide,
    grads,
    probe_sum,
    mid,
    patches,
):
    core, scan, live = meta[0], meta[1], meta[2]
    core_row = pl.multiple_of((1 - core) * (TILE + HALF), HALF)
    far_row = pl.multiple_of(core * (TILE + HALF), HALF)
    tall = low_lanes(W)
    short = low_lanes(HALF // 2)
    for part in range(4):
        wide[part, 0, HALF : HALF + TILE] = tile[part, :, :W]
        wide[part, 1, HALF : HALF + TILE] = tile[part, :, W:]
        right, left = from_right[part], from_left[part]
        wide[part, 2, HALF : HALF + W] = jnp.where(tall, right, swap(left))
        wide[part, 2, HALF + W : HALF + TILE] = jnp.where(tall, swap(right), left)
        for row, strip, corner_right, corner_left in (
            (core_row, from_core, core_right, core_left),
            (far_row, from_far, far_right, far_left),
        ):
            wide[part, 0, pl.ds(row, HALF)] = strip[part, :, :W]
            wide[part, 1, pl.ds(row, HALF)] = strip[part, :, W:]
            right, left = corner_right[part], corner_left[part]
            wide[part, 2, pl.ds(row, HALF // 2)] = jnp.where(short, right, swap(left))
            lower = pl.multiple_of(row + HALF // 2, HALF // 2)
            wide[part, 2, pl.ds(lower, HALF // 2)] = jnp.where(short, swap(right), left)

    forward_right = jnp.concatenate([right_high[...], right_high[...], right_low[...]], axis=0)
    inverse_right = jnp.concatenate([left_high[...], left_high[...], left_low[...]], axis=0)
    forward_left = jnp.concatenate([left_high[...], left_high[...], left_low[...]], axis=1)
    inverse_left = jnp.concatenate([right_high[...], right_high[...], right_low[...]], axis=1)

    def transform(real, imag):
        return times_left(forward_left, *times_right(real, imag, forward_right))

    def untransform(real, imag):
        return times_right(*times_left(inverse_left, real, imag), inverse_right)

    modes = range(MODES)
    lanes = lax.broadcasted_iota(jnp.int32, (W, W), 1)

    def visit(slot, carried):
        row = meta[3 + 2 * slot]
        col = meta[4 + 2 * slot]
        block = col // W
        shift = col - block * W
        after = jnp.where(block == 2, 0, block + 1)
        turn = jnp.where(shift == 0, 0, W - shift)
        for part in range(4):
            one = pltpu.roll(wide[part, block, pl.ds(row, W)], turn, 1)
            two = pltpu.roll(wide[part, after, pl.ds(row, W)], turn, 1)
            patches[part] = jnp.where(lanes < W - shift, one, two)
        near_real, near_imag = patches[0], patches[1]
        real = [probe[2 * m] * near_real - probe[2 * m + 1] * near_imag for m in modes]
        imag = [probe[2 * m] * near_imag + probe[2 * m + 1] * near_real for m in modes]
        real, imag = transform(real, imag)
        kr, ki = kernel_real[...], kernel_imag[...]
        real, imag = (
            [r * kr - i * ki for r, i in zip(real, imag)],
            [r * ki + i * kr for r, i in zip(real, imag)],
        )
        real, imag = untransform(real, imag)
        for m in modes:
            mid[2 * m] = real[m]
            mid[2 * m + 1] = imag[m]
        away_real, away_imag = patches[2], patches[3]
        real, imag = (
            [r * away_real - i * away_imag for r, i in zip(real, imag)],
            [r * away_imag + i * away_real for r, i in zip(real, imag)],
        )
        real, imag = transform(real, imag)
        intensity = functools.reduce(jnp.add, [r * r + i * i for r, i in zip(real, imag)])
        weight = jnp.where(slot < live, 2.0, 0.0).astype(F32)
        residual = (intensity - measured[slot]) * weight
        real, imag = untransform([r * residual for r in real], [i * residual for i in imag])
        grads[2, slot] = functools.reduce(
            jnp.add, [mid[2 * m] * real[m] + mid[2 * m + 1] * imag[m] for m in modes]
        )
        grads[3, slot] = functools.reduce(
            jnp.add, [mid[2 * m] * imag[m] - mid[2 * m + 1] * real[m] for m in modes]
        )
        real, imag = (
            [r * away_real + i * away_imag for r, i in zip(real, imag)],
            [i * away_real - r * away_imag for r, i in zip(real, imag)],
        )
        real, imag = transform(real, imag)
        real, imag = (
            [r * kr + i * ki for r, i in zip(real, imag)],
            [i * kr - r * ki for r, i in zip(real, imag)],
        )
        real, imag = untransform(real, imag)
        grads[0, slot] = functools.reduce(
            jnp.add, [probe[2 * m] * real[m] + probe[2 * m + 1] * imag[m] for m in modes]
        )
        grads[1, slot] = functools.reduce(
            jnp.add, [probe[2 * m] * imag[m] - probe[2 * m + 1] * real[m] for m in modes]
        )
        for m in modes:
            probe_sum[2 * m] += real[m] * near_real + imag[m] * near_imag
            probe_sum[2 * m + 1] += imag[m] * near_real - real[m] * near_imag
        return carried

    probe_sum[...] = jnp.zeros_like(probe_sum)
    lax.fori_loop(0, 2, visit, 0)

    places = lax.broadcasted_iota(jnp.int32, (8, W), 0)
    marks = jnp.zeros((8, W), F32)
    for k in range(4):
        marks = jnp.where(places == k, meta[3 + k].astype(F32), marks)
    for step, out in enumerate((out0, out1, out2, out3)):
        part = lax.rem(scan + step, 4)
        for slot in range(2):
            out[W * slot : W * (slot + 1)] = grads[part, slot]
        out[2 * W :] = marks
    count = jnp.zeros((8, W), F32) + live.astype(F32)
    for half, out in ((core, probe_keep), (1 - core, probe_send)):
        for k in range(MODES):
            out[W * k : W * (k + 1)] = probe_sum[half * MODES + k]
        out[MODES * W :] = count


def spread_body(keep, got, out):
    rows = out.shape[1] - 8
    count = keep[MODES * W :] + got[MODES * W :]
    for k in range(out.shape[0]):
        span = slice(k * rows, (k + 1) * rows)
        out[k, :rows] = keep[span] + got[span]
        out[k, rows:] = count


def place_body(one, two, three, four, chunks, to_left, to_right, keep, spread, wide):
    total = chunks[0]
    for k in range(1, chunks.shape[0]):
        total = total + chunks[k]
    for k in range(spread.shape[0]):
        spread[k] = total
    wide[...] = jnp.zeros_like(wide)
    lanes = lax.broadcasted_iota(jnp.int32, (W, W), 1)
    for message in (one, two, three, four):
        for slot in range(2):
            base = 2 * W + 2 * slot
            row = jnp.max(message[base : base + 1]).astype(jnp.int32)
            col = jnp.max(message[base + 1 : base + 2]).astype(jnp.int32)
            row = jnp.clip(row, 0, TILE)
            col = jnp.clip(col, 0, 3 * W - 1)
            block = col // W
            shift = col - block * W
            after = jnp.where(block == 2, 0, block + 1)
            turned = pltpu.roll(message[W * slot : W * (slot + 1)], shift, 1)
            wide[block, pl.ds(row, W)] += jnp.where(lanes >= shift, turned, 0.0)
            wide[after, pl.ds(row, W)] += jnp.where(lanes < shift, turned, 0.0)
    half = (TILE + 2 * HALF) // 2
    low = low_lanes(half)
    upper, lower = wide[2, :half], wide[2, half:]
    to_right[...] = jnp.where(low, upper, swap(lower))
    to_left[...] = jnp.where(low, swap(upper), lower)
    keep[0] = wide[0]
    keep[1] = wide[1]


def rows_body(meta, from_left, from_right, held, chunks, to_core, to_far, keep, spread, wide):
    total = chunks[0]
    for k in range(1, chunks.shape[0]):
        total = total + chunks[k]
    rows = spread.shape[1]
    mean = total[:rows] / total[rows : rows + 1]
    for k in range(spread.shape[0]):
        spread[k] = mean
    core = meta[0]
    half = (TILE + 2 * HALF) // 2
    low = low_lanes(half)
    left, right = from_left[...], from_right[...]
    wide[0, :half] = held[0, :half] + jnp.where(low, left, 0.0)
    wide[0, half:] = held[0, half:] + jnp.where(low, swap(left), 0.0)
    wide[1, :half] = held[1, :half] + jnp.where(low, 0.0, swap(right))
    wide[1, half:] = held[1, half:] + jnp.where(low, 0.0, right)
    core_row = pl.multiple_of((1 - core) * (TILE + HALF), HALF)
    far_row = pl.multiple_of(core * (TILE + HALF), HALF)
    for k in range(2):
        to_core[k] = wide[k, pl.ds(core_row, HALF)]
        to_far[k] = wide[k, pl.ds(far_row, HALF)]
        keep[k] = wide[k, HALF : HALF + TILE]


def finish_body(meta, from_core, from_far, held, out):
    core = meta[0]
    core_row = pl.multiple_of((1 - core) * (TILE - HALF), HALF)
    far_row = pl.multiple_of(core * (TILE - HALF), HALF)
    for k in range(2):
        span = slice(k * W, (k + 1) * W)
        out[:, span] = held[k]
        out[pl.ds(core_row, HALF), span] += from_core[k]
        out[pl.ds(far_row, HALF), span] += from_far[k]


def gather_body(meta, one, two, three, four, out):
    scan = meta[1]
    for step, part in enumerate((one, two, three, four)):
        out[lax.rem(scan + 4 - step, 4)] = part[...]


def halves_body(meta, mine, other, out):
    core = meta[0]
    out[core] = mine[...]
    out[1 - core] = other[...]


def tables():
    index = np.arange(W)
    angle = 2.0 * np.pi * ((index[:, None] * index[None, :]) % W) / W
    cos, sin = np.cos(angle) / np.sqrt(W), -np.sin(angle) / np.sqrt(W)
    right = np.block([[cos, sin], [-sin, cos]])
    arrays = []
    for table in (right, right.T):
        high = table.astype(BF16)
        low = (table - high.astype(np.float64)).astype(BF16)
        arrays += [high, low]
    return [jnp.asarray(a) for a in arrays]


def per_device(sizes, specimen, probe_modes, kernel_phase, offsets, live_counts, measured):
    nx, ntx, nsc = sizes
    core = lax.axis_index("core")
    scan = lax.axis_index("scan")
    starts = offsets[0, 0]
    rows = jnp.clip(starts[:, 0] + HALF, 0, TILE)
    cols = jnp.clip(starts[:, 1], -HALF, TILE - HALF)
    cols = jnp.where(cols < 0, cols + 3 * W, cols)
    meta = jnp.stack(
        [core, scan, live_counts[0, 0, 0], rows[0], cols[0], rows[1], cols[1]]
    ).astype(jnp.int32)

    def over_grid(target):
        pairs = []
        for x in range(nx):
            for c in range(2):
                for t in range(ntx):
                    x2, c2, t2 = target(x, c, t)
                    pairs.append(((x * 2 + c) * ntx + t, ((x2 % nx) * 2 + c2) * ntx + t2 % ntx))
        return lambda value: lax.ppermute(value, ("x", "core", "tx"), pairs)

    def across(x, c):
        return x + (1 if c else -1), 1 - c

    to_left = over_grid(lambda x, c, t: (x, c, t - 1))
    to_right = over_grid(lambda x, c, t: (x, c, t + 1))
    to_core = over_grid(lambda x, c, t: (x, 1 - c, t))
    to_far = over_grid(lambda x, c, t: (*across(x, c), t))
    core_left = over_grid(lambda x, c, t: (x, 1 - c, t - 1))
    core_right = over_grid(lambda x, c, t: (x, 1 - c, t + 1))
    far_left = over_grid(lambda x, c, t: (*across(x, c), t - 1))
    far_right = over_grid(lambda x, c, t: (*across(x, c), t + 1))

    def to_scan(value, step):
        return lax.ppermute(value, "scan", [(s, (s + step) % nsc) for s in range(nsc)])

    tile = specimen.reshape(4, TILE, TILE)
    edge, strip, corner = (4, W, W), (4, HALF, TILE), (4, HALF // 2, W)
    sent = call(
        pack_body,
        [edge, edge, strip, strip, corner, corner, corner, corner],
        (meta, tile),
        [SMEM, VMEM],
        name="pack",
    )
    moves = (to_left, to_right, to_core, to_far, core_left, core_right, far_left, far_right)
    rim = [move(value) for move, value in zip(moves, sent)]
    message = (2 * W + 8, W)
    share = (MODES * W + 8, W)
    outs = call(
        slots_body,
        [message] * 4 + [share] * 2,
        (
            meta,
            tile,
            *rim,
            probe_modes.reshape(2 * MODES, W, W),
            jnp.cos(kernel_phase),
            jnp.sin(kernel_phase),
            measured[0, 0],
            *tables(),
        ),
        [SMEM] + [VMEM] * 17,
        scratch=[
            pltpu.VMEM((4, 3, TILE + 2 * HALF, W), F32),
            pltpu.VMEM((4, 2, W, W), F32),
            pltpu.VMEM((2 * MODES, W, W), F32),
            pltpu.VMEM((2 * MODES, W, W), F32),
            pltpu.VMEM((4, W, W), F32),
        ],
        name="slots",
    )
    own, away, probe_send, probe_keep = outs[0], outs[1:4], outs[4], outs[5]
    probe_got = to_core(probe_send)
    arrived = [to_scan(value, step) for step, value in enumerate(away, 1)]
    group = nx * nsc
    rows_each = MODES * W // group
    (chunks,) = call(
        spread_body, [(group, rows_each + 8, W)], (probe_keep, probe_got), [VMEM] * 2, name="spread"
    )
    chunks = lax.all_to_all(chunks, ("x", "scan"), 0, 0)
    tall = TILE + 2 * HALF
    left, right, held, spread = call(
        place_body,
        [(tall // 2, W)] * 2 + [(2, tall, W), (ntx, rows_each + 8, W)],
        (own, *arrived, chunks),
        [VMEM] * 5,
        scratch=[pltpu.VMEM((3, tall, W), F32)],
        name="place",
    )
    left, right = to_left(left), to_right(right)
    spread = lax.all_to_all(spread, "tx", 0, 0)
    near, far, held, spread = call(
        rows_body,
        [(2, HALF, W)] * 2 + [(2, TILE, W), (group, rows_each, W)],
        (meta, right, left, held, spread),
        [SMEM] + [VMEM] * 4,
        scratch=[pltpu.VMEM((2, tall, W), F32)],
        name="rows",
    )
    near, far = to_core(near), to_far(far)
    mine = lax.all_to_all(spread, ("x", "scan"), 0, 0).reshape(MODES * W, W)
    (quarter,) = call(
        finish_body, [(TILE, TILE)], (meta, near, far, held), [SMEM] + [VMEM] * 3, name="finish"
    )
    quarters = [quarter] + [to_scan(quarter, step) for step in range(1, nsc)]
    other = to_core(mine)
    (probe_grad,) = call(
        halves_body, [(2, MODES * W, W)], (meta, mine, other), [SMEM] + [VMEM] * 2, name="halves"
    )
    (object_grad,) = call(
        gather_body, [(4, TILE, TILE)], (meta, *quarters), [SMEM] + [VMEM] * 4, name="gather"
    )
    return object_grad.reshape(specimen.shape), probe_grad.reshape(probe_modes.shape)


def solution(mesh):
    ny, ntx, nsc = mesh.devices.shape
    split = Mesh(mesh.devices.reshape(ny // 2, 2, ntx, nsc), ("x", "core", "tx", "scan"))
    rows = ("x", "core")
    placed = (
        P(None, None, rows, "tx"),
        P(),
        P(),
        P(rows, "tx", "scan", None),
        P(rows, "tx", "scan"),
        P(rows, "tx", "scan", None, None),
    )
    return jax.shard_map(
        functools.partial(per_device, (ny // 2, ntx, nsc)),
        mesh=split,
        in_specs=placed,
        out_specs=(P(None, None, rows, "tx"), P()),
        check_vma=False,
    )
```

```python
import functools

import jax
import jax.numpy as jnp
import numpy as np
from jax import lax
from jax.experimental import pallas as pl
from jax.experimental.pallas import tpu as pltpu
from jax.sharding import Mesh
from jax.sharding import PartitionSpec as P

F32 = jnp.float32
BF16 = jnp.bfloat16
VMEM = pl.BlockSpec(memory_space=pltpu.VMEM)
SMEM = pl.BlockSpec(memory_space=pltpu.SMEM)
ANY = pl.BlockSpec(memory_space=pl.ANY)
LONG = 10**10
PARAMS = pltpu.CompilerParams(vmem_limit_bytes=48 * 1024 * 1024)
W = 128
HALF = 64
TILE = 256
MODES = 4


def call(body, outs, args, specs, scratch=(), name=None, flops=0):
    return pl.pallas_call(
        body,
        out_shape=[jax.ShapeDtypeStruct(shape, F32) for shape in outs],
        in_specs=specs,
        out_specs=[VMEM] * len(outs),
        scratch_shapes=list(scratch),
        compiler_params=PARAMS,
        cost_estimate=pl.CostEstimate(flops=flops, bytes_accessed=0, transcendentals=0) if flops else None,
        name=name,
    )(*args)


def low_lanes(rows):
    return lax.broadcasted_iota(jnp.int32, (rows, W), 1) < HALF


def swap(x):
    return pltpu.roll(x, HALF, 1)


def rim_rows(core, last):
    return pl.multiple_of((1 - core) * last, HALF), pl.multiple_of(core * last, HALF)


def fold_corner(rows, left, right):
    short = low_lanes(HALF // 2)
    upper, lower = rows[: HALF // 2], rows[HALF // 2 :]
    left[...] = jnp.where(short, upper[:, :W], swap(lower[:, :W]))
    right[...] = jnp.where(short, swap(upper[:, W:]), lower[:, W:])


def pack_body(tile, to_core, to_far, far_left, far_right):
    core_row, far_row = rim_rows(lax.axis_index("core"), TILE - HALF)
    for part in range(4):
        to_core[part] = tile[part, pl.ds(core_row, HALF), :]
        rows = tile[part, pl.ds(far_row, HALF), :]
        to_far[part] = rows
        fold_corner(rows, far_left.at[part], far_right.at[part])


def sides_body(tile, from_core, to_left, to_right):
    wide = low_lanes(W)
    for part in range(4):
        first, second = tile[part, :W, :W], tile[part, W:, :W]
        to_left[part, :W] = jnp.where(wide, first, swap(second))
        first, second = tile[part, :W, W:], tile[part, W:, W:]
        to_right[part, :W] = jnp.where(wide, swap(first), second)
        corners = slice(W, W + HALF // 2)
        fold_corner(from_core[part], to_left.at[part, corners], to_right.at[part, corners])


def phase_body(phase, after, real, imag):
    real[...] = jnp.cos(phase[...])
    imag[...] = jnp.sin(phase[...])


def halves(x):
    high = x.astype(BF16)
    return high, (x - high.astype(F32)).astype(BF16)


def times_right(real, imag, table):
    outs = ([], [])
    for k in range(len(real)):
        high, low = halves(jnp.concatenate([real[k], imag[k]], axis=1))
        out = jnp.dot(jnp.concatenate([high, low, high], axis=1), table, preferred_element_type=F32)
        outs[0].append(out[:, :W])
        outs[1].append(out[:, W:])
    return outs


def times_left(table, real, imag):
    outs = ([], [])
    for k in range(0, len(real), 2):
        high, low = halves(
            jnp.concatenate(
                [jnp.concatenate(real[k : k + 2], axis=1), jnp.concatenate(imag[k : k + 2], axis=1)],
                axis=0,
            )
        )
        out = jnp.dot(table, jnp.concatenate([high, low, high], axis=0), preferred_element_type=F32)
        for m in range(2):
            outs[0].append(out[:W, W * m : W * (m + 1)])
            outs[1].append(out[W:, W * m : W * (m + 1)])
    return outs


def slots_body(
    offsets,
    live_counts,
    tile,
    from_right,
    from_left,
    from_core,
    from_far,
    far_right,
    far_left,
    probe,
    kernel_real,
    kernel_imag,
    measured,
    right_high,
    right_low,
    left_high,
    left_low,
    out0,
    out1,
    out2,
    out3,
    probe_send,
    probe_keep,
    wide,
    grads,
    probe_sum,
    mid,
    patches,
):
    core, scan = lax.axis_index("core"), lax.axis_index("scan")
    live = live_counts[0, 0, 0]
    core_row, far_row = rim_rows(core, TILE + HALF)
    tall = low_lanes(W)
    short = low_lanes(HALF // 2)
    for part in range(4):
        wide[part, 0, HALF : HALF + TILE] = tile[part, :, :W]
        wide[part, 1, HALF : HALF + TILE] = tile[part, :, W:]
        right, left = from_right[part, :W], from_left[part, :W]
        wide[part, 2, HALF : HALF + W] = jnp.where(tall, right, swap(left))
        wide[part, 2, HALF + W : HALF + TILE] = jnp.where(tall, swap(right), left)
        for row, strip, right, left in (
            (core_row, from_core, from_right[part, W:], from_left[part, W:]),
            (far_row, from_far, far_right[part], far_left[part]),
        ):
            wide[part, 0, pl.ds(row, HALF)] = strip[part, :, :W]
            wide[part, 1, pl.ds(row, HALF)] = strip[part, :, W:]
            wide[part, 2, pl.ds(row, HALF // 2)] = jnp.where(short, right, swap(left))
            lower = pl.multiple_of(row + HALF // 2, HALF // 2)
            wide[part, 2, pl.ds(lower, HALF // 2)] = jnp.where(short, swap(right), left)

    def corner(slot):
        row = jnp.clip(offsets[0, 0, slot, 0] + HALF, 0, TILE)
        col = jnp.clip(offsets[0, 0, slot, 1], -HALF, TILE - HALF)
        return row, jnp.where(col < 0, col + 3 * W, col)

    forward_right = jnp.concatenate([right_high[...], right_high[...], right_low[...]], axis=0)
    inverse_right = jnp.concatenate([left_high[...], left_high[...], left_low[...]], axis=0)
    forward_left = jnp.concatenate([left_high[...], left_high[...], left_low[...]], axis=1)
    inverse_left = jnp.concatenate([right_high[...], right_high[...], right_low[...]], axis=1)

    def transform(real, imag):
        return times_left(forward_left, *times_right(real, imag, forward_right))

    def untransform(real, imag):
        return times_right(*times_left(inverse_left, real, imag), inverse_right)

    modes = range(MODES)
    lanes = lax.broadcasted_iota(jnp.int32, (W, W), 1)

    for slot in range(2):
        row, col = corner(slot)
        block = col // W
        shift = col - block * W
        after = jnp.where(block == 2, 0, block + 1)
        turn = jnp.where(shift == 0, 0, W - shift)
        for part in range(4):
            one = pltpu.roll(wide[part, block, pl.ds(row, W)], turn, 1)
            two = pltpu.roll(wide[part, after, pl.ds(row, W)], turn, 1)
            patches[4 * slot + part] = jnp.where(lanes < W - shift, one, two)
    slots = range(2)
    pairs = [(slot, m) for slot in slots for m in modes]

    def patch(part):
        return [patches[4 * slot + part] for slot in slots]

    def times(real, imag, by_real, by_imag):
        return (
            [r * by_real[s] - i * by_imag[s] for (s, m), r, i in zip(pairs, real, imag)],
            [r * by_imag[s] + i * by_real[s] for (s, m), r, i in zip(pairs, real, imag)],
        )

    def times_conj(real, imag, by_real, by_imag):
        return (
            [r * by_real[s] + i * by_imag[s] for (s, m), r, i in zip(pairs, real, imag)],
            [i * by_real[s] - r * by_imag[s] for (s, m), r, i in zip(pairs, real, imag)],
        )

    def total(terms):
        return [functools.reduce(jnp.add, terms[MODES * s : MODES * (s + 1)]) for s in slots]

    near_real, near_imag = patch(0), patch(1)
    real, imag = times(
        [probe[2 * m] for s, m in pairs], [probe[2 * m + 1] for s, m in pairs], near_real, near_imag
    )
    real, imag = transform(real, imag)
    kr, ki = [kernel_real[...]] * 2, [kernel_imag[...]] * 2
    real, imag = times(real, imag, kr, ki)
    real, imag = untransform(real, imag)
    for n in range(2 * MODES):
        mid[2 * n] = real[n]
        mid[2 * n + 1] = imag[n]
    away_real, away_imag = patch(2), patch(3)
    real, imag = times(real, imag, away_real, away_imag)
    real, imag = transform(real, imag)
    intensity = total([r * r + i * i for r, i in zip(real, imag)])
    residual = [
        (intensity[s] - measured[s]) * jnp.where(s < live, 2.0, 0.0).astype(F32) for s in slots
    ]
    real = [r * residual[s] for (s, m), r in zip(pairs, real)]
    imag = [i * residual[s] for (s, m), i in zip(pairs, imag)]
    real, imag = untransform(real, imag)
    both = range(2 * MODES)
    grad_real = total([mid[2 * n] * real[n] + mid[2 * n + 1] * imag[n] for n in both])
    grad_imag = total([mid[2 * n] * imag[n] - mid[2 * n + 1] * real[n] for n in both])
    for s in slots:
        grads[2, s] = grad_real[s]
        grads[3, s] = grad_imag[s]
    real, imag = times_conj(real, imag, patch(2), patch(3))
    real, imag = transform(real, imag)
    real, imag = times_conj(real, imag, kr, ki)
    real, imag = untransform(real, imag)
    grad_real = total([probe[2 * m] * real[n] + probe[2 * m + 1] * imag[n] for n, (s, m) in enumerate(pairs)])
    grad_imag = total([probe[2 * m] * imag[n] - probe[2 * m + 1] * real[n] for n, (s, m) in enumerate(pairs)])
    for s in slots:
        grads[0, s] = grad_real[s]
        grads[1, s] = grad_imag[s]
    real, imag = times_conj(real, imag, patch(0), patch(1))
    for m in modes:
        probe_sum[2 * m] = real[m] + real[MODES + m]
        probe_sum[2 * m + 1] = imag[m] + imag[MODES + m]

    places = lax.broadcasted_iota(jnp.int32, (8, W), 0)
    marks = jnp.zeros((8, W), F32)
    for k, value in enumerate((*corner(0), *corner(1))):
        marks = jnp.where(places == k, value.astype(F32), marks)
    for step, out in enumerate((out0, out1, out2, out3)):
        part = lax.rem(scan + step, 4)
        for slot in range(2):
            out[W * slot : W * (slot + 1)] = grads[part, slot]
        out[2 * W :] = marks
    count = jnp.zeros((8, W), F32) + live.astype(F32)
    for half, out in ((core, probe_keep), (1 - core, probe_send)):
        for k in range(MODES):
            out[W * k : W * (k + 1)] = probe_sum[half * MODES + k]
        out[MODES * W :] = count


def spread_body(keep, got, out):
    rows = out.shape[1] - 8
    count = keep[MODES * W :] + got[MODES * W :]
    for k in range(out.shape[0]):
        span = slice(k * rows, (k + 1) * rows)
        out[k, :rows] = keep[span] + got[span]
        out[k, rows:] = count


def total_of(chunks):
    total = chunks[0]
    for k in range(1, chunks.shape[0]):
        total = total + chunks[k]
    return total


def sum_body(chunks, after, spread):
    total = total_of(chunks)
    for k in range(spread.shape[0]):
        spread[k] = total


def mean_body(chunks, after, spread):
    total = total_of(chunks)
    rows = spread.shape[1]
    mean = total[:rows] / total[rows : rows + 1]
    for k in range(spread.shape[0]):
        spread[k] = mean


def place_body(one, two, three, four, wide):
    wide[...] = jnp.zeros_like(wide)
    lanes = lax.broadcasted_iota(jnp.int32, (W, W), 1)
    for message in (one, two, three, four):
        for slot in range(2):
            base = 2 * W + 2 * slot
            row = jnp.max(message[base : base + 1]).astype(jnp.int32)
            col = jnp.max(message[base + 1 : base + 2]).astype(jnp.int32)
            row = jnp.clip(row, 0, TILE)
            col = jnp.clip(col, 0, 3 * W - 1)
            block = col // W
            shift = col - block * W
            after = jnp.where(block == 2, 0, block + 1)
            turned = pltpu.roll(message[W * slot : W * (slot + 1)], shift, 1)
            wide[block, pl.ds(row, W)] += jnp.where(lanes >= shift, turned, 0.0)
            wide[after, pl.ds(row, W)] += jnp.where(lanes < shift, turned, 0.0)


def edges_body(wide, after, to_left, to_right):
    half = (TILE + 2 * HALF) // 2
    low = low_lanes(half)
    upper, lower = wide[2, :half], wide[2, half:]
    to_right[...] = jnp.where(low, upper, swap(lower))
    to_left[...] = jnp.where(low, swap(upper), lower)


def rows_body(from_left, from_right, held, to_core, to_far, keep, wide):
    half = (TILE + 2 * HALF) // 2
    low = low_lanes(half)
    left, right = from_left[...], from_right[...]
    wide[0, :half] = held[0, :half] + jnp.where(low, left, 0.0)
    wide[0, half:] = held[0, half:] + jnp.where(low, swap(left), 0.0)
    wide[1, :half] = held[1, :half] + jnp.where(low, 0.0, swap(right))
    wide[1, half:] = held[1, half:] + jnp.where(low, 0.0, right)
    core_row, far_row = rim_rows(lax.axis_index("core"), TILE + HALF)
    for k in range(2):
        to_core[k] = wide[k, pl.ds(core_row, HALF)]
        to_far[k] = wide[k, pl.ds(far_row, HALF)]
        keep[k] = wide[k, HALF : HALF + TILE]


def finish_body(from_core, from_far, held, out):
    core_row, far_row = rim_rows(lax.axis_index("core"), TILE - HALF)
    for k in range(2):
        span = slice(k * W, (k + 1) * W)
        out[:, span] = held[k]
        out[pl.ds(core_row, HALF), span] += from_core[k]
        out[pl.ds(far_row, HALF), span] += from_far[k]


def gather_body(one, two, three, four, out):
    scan = lax.axis_index("scan")
    for step, part in enumerate((one, two, three, four)):
        out[lax.rem(scan + 4 - step, 4)] = part[...]


def halves_body(mine, other, out):
    core = lax.axis_index("core")
    out[core] = mine[...]
    out[1 - core] = other[...]


def tables():
    index = np.arange(W)
    angle = 2.0 * np.pi * ((index[:, None] * index[None, :]) % W) / W
    cos, sin = np.cos(angle) / np.sqrt(W), -np.sin(angle) / np.sqrt(W)
    right = np.block([[cos, sin], [-sin, cos]])
    arrays = []
    for table in (right, right.T):
        high = table.astype(BF16)
        low = (table - high.astype(np.float64)).astype(BF16)
        arrays += [high, low]
    return [jnp.asarray(a) for a in arrays]


def run_slots(*args):
    message = (2 * W + 8, W)
    share = (MODES * W + 8, W)
    return call(
        slots_body,
        [message] * 4 + [share] * 2,
        (*args, *tables()),
        [SMEM] * 2 + [VMEM] * 15,
        scratch=[
            pltpu.VMEM((4, 3, TILE + 2 * HALF, W), F32),
            pltpu.VMEM((4, 2, W, W), F32),
            pltpu.VMEM((2 * MODES, W, W), F32),
            pltpu.VMEM((4 * MODES, W, W), F32),
            pltpu.VMEM((8, W, W), F32),
        ],
        name="slots",
    )


def per_device(sizes, specimen, probe_modes, kernel_phase, offsets, live_counts, measured):
    nx, ntx, nsc = sizes

    def over_grid(target):
        pairs = []
        for x in range(nx):
            for c in range(2):
                for t in range(ntx):
                    x2, c2, t2 = target(x, c, t)
                    pairs.append(((x * 2 + c) * ntx + t, ((x2 % nx) * 2 + c2) * ntx + t2 % ntx))
        return lambda value: lax.ppermute(value, ("x", "core", "tx"), pairs)

    def across(x, c):
        return x + (1 if c else -1), 1 - c

    to_left = over_grid(lambda x, c, t: (x, c, t - 1))
    to_right = over_grid(lambda x, c, t: (x, c, t + 1))
    to_core = over_grid(lambda x, c, t: (x, 1 - c, t))
    to_far = over_grid(lambda x, c, t: (*across(x, c), t))
    far_left = over_grid(lambda x, c, t: (*across(x, c), t - 1))
    far_right = over_grid(lambda x, c, t: (*across(x, c), t + 1))

    def to_scan(value, step):
        return lax.ppermute(value, "scan", [(s, (s + step) % nsc) for s in range(nsc)])

    tile = specimen.reshape(4, TILE, TILE)
    strip, corner, side = (4, HALF, TILE), (4, HALF // 2, W), (4, W + HALF // 2, W)
    near, far, left, right = call(
        pack_body, [strip, strip, corner, corner], (tile,), [VMEM], name="pack"
    )
    marker = far
    from_core = to_core(near)
    from_far, corner_right, corner_left = to_far(far), far_left(left), far_right(right)
    left, right = call(
        sides_body, [side, side], (tile, from_core), [VMEM] * 2, name="sides", flops=LONG
    )
    from_right, from_left = to_left(left), to_right(right)
    kernel_real, kernel_imag = call(
        phase_body, [(W, W)] * 2, (kernel_phase, marker), [VMEM, ANY], name="phase", flops=10**9
    )
    outs = run_slots(
        offsets,
        live_counts,
        tile,
        from_right,
        from_left,
        from_core,
        from_far,
        corner_right,
        corner_left,
        probe_modes.reshape(2 * MODES, W, W),
        kernel_real,
        kernel_imag,
        measured[0, 0],
    )
    own, away, probe_send, probe_keep = outs[0], outs[1:4], outs[4], outs[5]
    arrived = [to_scan(value, step) for step, value in enumerate(away, 1)]
    probe_got = to_core(probe_send)
    group = nx * nsc
    rows_each = MODES * W // group
    (chunks,) = call(
        spread_body,
        [(group, rows_each + 8, W)],
        (probe_keep, probe_got),
        [VMEM] * 2,
        name="spread",
        flops=LONG,
    )
    chunks = lax.all_to_all(chunks, ("x", "scan"), 0, 0)
    tall = TILE + 2 * HALF
    (held,) = call(
        place_body, [(3, tall, W)], (own, *arrived), [VMEM] * 4, name="place", flops=LONG
    )
    left, right = call(
        edges_body, [(tall // 2, W)] * 2, (held, chunks), [VMEM, ANY], name="edges"
    )
    left, right = to_left(left), to_right(right)
    near, far, held = call(
        rows_body,
        [(2, HALF, W)] * 2 + [(2, TILE, W)],
        (right, left, held),
        [VMEM] * 3,
        scratch=[pltpu.VMEM((2, tall, W), F32)],
        name="rows",
        flops=LONG,
    )
    (spread,) = call(
        sum_body,
        [(ntx, rows_each + 8, W)],
        (chunks, near),
        [VMEM, ANY],
        name="sum",
        flops=LONG,
    )
    near, far = to_core(near), to_far(far)
    spread = lax.all_to_all(spread, "tx", 0, 0)
    (quarter,) = call(
        finish_body, [(TILE, TILE)], (near, far, held), [VMEM] * 3, name="finish", flops=LONG
    )
    (spread,) = call(
        mean_body,
        [(group, rows_each, W)],
        (spread, quarter),
        [VMEM, ANY],
        name="mean",
        flops=LONG,
    )
    mine = lax.all_to_all(spread, ("x", "scan"), 0, 0).reshape(MODES * W, W)
    quarters = [quarter] + [to_scan(quarter, step) for step in range(1, nsc)]
    other = to_core(mine)
    (probe_grad,) = call(
        halves_body, [(2, MODES * W, W)], (mine, other), [VMEM] * 2, name="halves", flops=LONG
    )
    (object_grad,) = call(gather_body, [(4, TILE, TILE)], quarters, [VMEM] * 4, name="gather", flops=LONG)
    return object_grad.reshape(specimen.shape), probe_grad.reshape(probe_modes.shape)


def solution(mesh):
    ny, ntx, nsc = mesh.devices.shape
    split = Mesh(mesh.devices.reshape(ny // 2, 2, ntx, nsc), ("x", "core", "tx", "scan"))
    rows = ("x", "core")
    placed = (
        P(None, None, rows, "tx"),
        P(),
        P(),
        P(rows, "tx", "scan", None),
        P(rows, "tx", "scan"),
        P(rows, "tx", "scan", None, None),
    )
    return jax.shard_map(
        functools.partial(per_device, (ny // 2, ntx, nsc)),
        mesh=split,
        in_specs=placed,
        out_specs=(P(None, None, rows, "tx"), P()),
        check_vma=False,
    )
```

```python
import functools

import jax
import jax.numpy as jnp
import numpy as np
from jax import lax
from jax.experimental import pallas as pl
from jax.experimental.pallas import tpu as pltpu
from jax.sharding import Mesh
from jax.sharding import PartitionSpec as P

F32 = jnp.float32
BF16 = jnp.bfloat16
VMEM = pl.BlockSpec(memory_space=pltpu.VMEM)
SMEM = pl.BlockSpec(memory_space=pltpu.SMEM)
ANY = pl.BlockSpec(memory_space=pl.ANY)
LONG = 10**10
PARAMS = pltpu.CompilerParams(vmem_limit_bytes=48 * 1024 * 1024)
W = 128
HALF = 64
TILE = 256
MODES = 4


def call(body, outs, args, specs, scratch=(), name=None, flops=0):
    return pl.pallas_call(
        body,
        out_shape=[jax.ShapeDtypeStruct(shape, F32) for shape in outs],
        in_specs=specs,
        out_specs=[VMEM] * len(outs),
        scratch_shapes=list(scratch),
        compiler_params=PARAMS,
        cost_estimate=pl.CostEstimate(flops=flops, bytes_accessed=0, transcendentals=0) if flops else None,
        name=name,
    )(*args)


def low_lanes(rows):
    return lax.broadcasted_iota(jnp.int32, (rows, W), 1) < HALF


def swap(x):
    return pltpu.roll(x, HALF, 1)


def rim_rows(core, last):
    return pl.multiple_of((1 - core) * last, HALF), pl.multiple_of(core * last, HALF)


def fold_corner(rows, left, right):
    short = low_lanes(HALF // 2)
    upper, lower = rows[: HALF // 2], rows[HALF // 2 :]
    left[...] = jnp.where(short, upper[:, :W], swap(lower[:, :W]))
    right[...] = jnp.where(short, swap(upper[:, W:]), lower[:, W:])


def sides_body(tile, to_left, to_right):
    wide = low_lanes(W)
    for part in range(4):
        first, second = tile[part, :W, :W], tile[part, W:, :W]
        to_left[part] = jnp.where(wide, first, swap(second))
        first, second = tile[part, :W, W:], tile[part, W:, W:]
        to_right[part] = jnp.where(wide, swap(first), second)


def strips_body(tile, after, to_core, to_far, far_left, far_right):
    core_row, far_row = rim_rows(lax.axis_index("core"), TILE - HALF)
    for part in range(4):
        to_core[part] = tile[part, pl.ds(core_row, HALF), :]
        rows = tile[part, pl.ds(far_row, HALF), :]
        to_far[part] = rows
        fold_corner(rows, far_left.at[part], far_right.at[part])


def corners_body(from_right, from_left, far, far_right, far_left, out):
    core = lax.axis_index("core")
    low = low_lanes(HALF)
    span = pl.ds(pl.multiple_of((1 - core) * HALF, HALF), HALF)
    for part in range(4):
        right, left = from_right[part, span], from_left[part, span]
        right = jnp.where(core == 0, swap(right), right)
        left = jnp.where(core == 0, left, swap(left))
        out[part] = jnp.where(low, right, left)


def phase_body(phase, right, left, real, imag):
    real[...] = jnp.cos(phase[...])
    imag[...] = jnp.sin(phase[...])


def halves(x):
    high = x.astype(BF16)
    return high, (x - high.astype(F32)).astype(BF16)


def times_right(real, imag, table):
    outs = ([], [])
    for k in range(len(real)):
        high, low = halves(jnp.concatenate([real[k], imag[k]], axis=1))
        out = jnp.dot(jnp.concatenate([high, low, high], axis=1), table, preferred_element_type=F32)
        outs[0].append(out[:, :W])
        outs[1].append(out[:, W:])
    return outs


def times_left(table, real, imag):
    outs = ([], [])
    for k in range(0, len(real), 2):
        high, low = halves(
            jnp.concatenate(
                [jnp.concatenate(real[k : k + 2], axis=1), jnp.concatenate(imag[k : k + 2], axis=1)],
                axis=0,
            )
        )
        out = jnp.dot(table, jnp.concatenate([high, low, high], axis=0), preferred_element_type=F32)
        for m in range(2):
            outs[0].append(out[:W, W * m : W * (m + 1)])
            outs[1].append(out[W:, W * m : W * (m + 1)])
    return outs


def slots_body(
    starts,
    live_counts,
    tile,
    from_right,
    from_left,
    from_core,
    from_far,
    far_right,
    far_left,
    corners,
    probe,
    kernel_real,
    kernel_imag,
    measured,
    right_high,
    right_low,
    left_high,
    left_low,
    out0,
    out1,
    out2,
    out3,
    probe_send,
    probe_keep,
    wide,
    grads,
    probe_sum,
    mid,
    patches,
):
    core, scan = lax.axis_index("core"), lax.axis_index("scan")
    live = live_counts[0, 0, 0]
    core_row, far_row = rim_rows(core, TILE + HALF)
    tall = low_lanes(W)
    short = low_lanes(HALF // 2)
    for part in range(4):
        wide[part, 0, HALF : HALF + TILE] = tile[part, :, :W]
        wide[part, 1, HALF : HALF + TILE] = tile[part, :, W:]
        right, left = from_right[part], from_left[part]
        wide[part, 2, HALF : HALF + W] = jnp.where(tall, right, swap(left))
        wide[part, 2, HALF + W : HALF + TILE] = jnp.where(tall, swap(right), left)
        for row, strip in ((core_row, from_core), (far_row, from_far)):
            wide[part, 0, pl.ds(row, HALF)] = strip[part, :, :W]
            wide[part, 1, pl.ds(row, HALF)] = strip[part, :, W:]
        wide[part, 2, pl.ds(core_row, HALF)] = corners[part]
        right, left = far_right[part], far_left[part]
        wide[part, 2, pl.ds(far_row, HALF // 2)] = jnp.where(short, right, swap(left))
        lower = pl.multiple_of(far_row + HALF // 2, HALF // 2)
        wide[part, 2, pl.ds(lower, HALF // 2)] = jnp.where(short, swap(right), left)

    def corner(slot):
        return starts[2 * slot], starts[2 * slot + 1]

    forward_right = jnp.concatenate([right_high[...], right_high[...], right_low[...]], axis=0)
    inverse_right = jnp.concatenate([left_high[...], left_high[...], left_low[...]], axis=0)
    forward_left = jnp.concatenate([left_high[...], left_high[...], left_low[...]], axis=1)
    inverse_left = jnp.concatenate([right_high[...], right_high[...], right_low[...]], axis=1)

    def transform(real, imag):
        return times_left(forward_left, *times_right(real, imag, forward_right))

    def untransform(real, imag):
        return times_right(*times_left(inverse_left, real, imag), inverse_right)

    modes = range(MODES)
    lanes = lax.broadcasted_iota(jnp.int32, (W, W), 1)

    for slot in range(2):
        row, col = corner(slot)
        block = col // W
        shift = col - block * W
        after = jnp.where(block == 2, 0, block + 1)
        turn = jnp.where(shift == 0, 0, W - shift)
        for part in range(4):
            one = pltpu.roll(wide[part, block, pl.ds(row, W)], turn, 1)
            two = pltpu.roll(wide[part, after, pl.ds(row, W)], turn, 1)
            patches[4 * slot + part] = jnp.where(lanes < W - shift, one, two)
    slots = range(2)
    pairs = [(slot, m) for slot in slots for m in modes]

    def patch(part):
        return [patches[4 * slot + part] for slot in slots]

    def times(real, imag, by_real, by_imag):
        return (
            [r * by_real[s] - i * by_imag[s] for (s, m), r, i in zip(pairs, real, imag)],
            [r * by_imag[s] + i * by_real[s] for (s, m), r, i in zip(pairs, real, imag)],
        )

    def times_conj(real, imag, by_real, by_imag):
        return (
            [r * by_real[s] + i * by_imag[s] for (s, m), r, i in zip(pairs, real, imag)],
            [i * by_real[s] - r * by_imag[s] for (s, m), r, i in zip(pairs, real, imag)],
        )

    def total(terms):
        return [functools.reduce(jnp.add, terms[MODES * s : MODES * (s + 1)]) for s in slots]

    near_real, near_imag = patch(0), patch(1)
    real, imag = times(
        [probe[2 * m] for s, m in pairs], [probe[2 * m + 1] for s, m in pairs], near_real, near_imag
    )
    real, imag = transform(real, imag)
    kr, ki = [kernel_real[...]] * 2, [kernel_imag[...]] * 2
    real, imag = times(real, imag, kr, ki)
    real, imag = untransform(real, imag)
    for n in range(2 * MODES):
        mid[2 * n] = real[n]
        mid[2 * n + 1] = imag[n]
    away_real, away_imag = patch(2), patch(3)
    real, imag = times(real, imag, away_real, away_imag)
    real, imag = transform(real, imag)
    intensity = total([r * r + i * i for r, i in zip(real, imag)])
    residual = [
        (intensity[s] - measured[s]) * jnp.where(s < live, 2.0, 0.0).astype(F32) for s in slots
    ]
    real = [r * residual[s] for (s, m), r in zip(pairs, real)]
    imag = [i * residual[s] for (s, m), i in zip(pairs, imag)]
    real, imag = untransform(real, imag)
    both = range(2 * MODES)
    grad_real = total([mid[2 * n] * real[n] + mid[2 * n + 1] * imag[n] for n in both])
    grad_imag = total([mid[2 * n] * imag[n] - mid[2 * n + 1] * real[n] for n in both])
    for s in slots:
        grads[2, s] = grad_real[s]
        grads[3, s] = grad_imag[s]
    real, imag = times_conj(real, imag, patch(2), patch(3))
    real, imag = transform(real, imag)
    real, imag = times_conj(real, imag, kr, ki)
    real, imag = untransform(real, imag)
    grad_real = total([probe[2 * m] * real[n] + probe[2 * m + 1] * imag[n] for n, (s, m) in enumerate(pairs)])
    grad_imag = total([probe[2 * m] * imag[n] - probe[2 * m + 1] * real[n] for n, (s, m) in enumerate(pairs)])
    for s in slots:
        grads[0, s] = grad_real[s]
        grads[1, s] = grad_imag[s]
    real, imag = times_conj(real, imag, patch(0), patch(1))
    for m in modes:
        probe_sum[2 * m] = real[m] + real[MODES + m]
        probe_sum[2 * m + 1] = imag[m] + imag[MODES + m]

    places = lax.broadcasted_iota(jnp.int32, (8, W), 0)
    marks = jnp.zeros((8, W), F32)
    for k, value in enumerate((*corner(0), *corner(1))):
        marks = jnp.where(places == k, value.astype(F32), marks)
    for step, out in enumerate((out0, out1, out2, out3)):
        part = lax.rem(scan + step, 4)
        for slot in range(2):
            out[W * slot : W * (slot + 1)] = grads[part, slot]
        out[2 * W :] = marks
    count = jnp.zeros((8, W), F32) + live.astype(F32)
    for half, out in ((core, probe_keep), (1 - core, probe_send)):
        for k in range(MODES):
            out[W * k : W * (k + 1)] = probe_sum[half * MODES + k]
        out[MODES * W :] = count


def spread_body(keep, got, out):
    rows = out.shape[1] - 8
    count = keep[MODES * W :] + got[MODES * W :]
    for k in range(out.shape[0]):
        span = slice(k * rows, (k + 1) * rows)
        out[k, :rows] = keep[span] + got[span]
        out[k, rows:] = count


def sum_body(chunks, after, out):
    out[...] = functools.reduce(jnp.add, [chunks[k] for k in range(chunks.shape[0])])


def group_body(zero, one, two, three, after, out):
    out[...] = (zero[...] + one[...]) + (two[...] + three[...])


def mean_body(own, got, spread):
    total = own[...] + got[...]
    rows = spread.shape[1]
    mean = total[:rows] / total[rows : rows + 1]
    for k in range(spread.shape[0]):
        spread[k] = mean


def place_body(one, two, three, four, to_left, to_right, wide):
    wide[...] = jnp.zeros_like(wide)
    lanes = lax.broadcasted_iota(jnp.int32, (W, W), 1)
    for message in (one, two, three, four):
        for slot in range(2):
            base = 2 * W + 2 * slot
            row = jnp.max(message[base : base + 1]).astype(jnp.int32)
            col = jnp.max(message[base + 1 : base + 2]).astype(jnp.int32)
            row = jnp.clip(row, 0, TILE)
            col = jnp.clip(col, 0, 3 * W - 1)
            block = col // W
            shift = col - block * W
            after = jnp.where(block == 2, 0, block + 1)
            turned = pltpu.roll(message[W * slot : W * (slot + 1)], shift, 1)
            wide[block, pl.ds(row, W)] += jnp.where(lanes >= shift, turned, 0.0)
            wide[after, pl.ds(row, W)] += jnp.where(lanes < shift, turned, 0.0)
    half = (TILE + 2 * HALF) // 2
    low = low_lanes(half)
    upper, lower = wide[2, :half], wide[2, half:]
    to_right[...] = jnp.where(low, upper, swap(lower))
    to_left[...] = jnp.where(low, swap(upper), lower)


def rows_body(from_left, from_right, held, after, to_core, to_far, keep, wide):
    half = (TILE + 2 * HALF) // 2
    low = low_lanes(half)
    left, right = from_left[...], from_right[...]
    wide[0, :half] = held[0, :half] + jnp.where(low, left, 0.0)
    wide[0, half:] = held[0, half:] + jnp.where(low, swap(left), 0.0)
    wide[1, :half] = held[1, :half] + jnp.where(low, 0.0, swap(right))
    wide[1, half:] = held[1, half:] + jnp.where(low, 0.0, right)
    core_row, far_row = rim_rows(lax.axis_index("core"), TILE + HALF)
    for k in range(2):
        to_core[k] = wide[k, pl.ds(core_row, HALF)]
        to_far[k] = wide[k, pl.ds(far_row, HALF)]
        keep[k] = wide[k, HALF : HALF + TILE]


def finish_body(from_core, from_far, held, after, out):
    core_row, far_row = rim_rows(lax.axis_index("core"), TILE - HALF)
    for k in range(2):
        span = slice(k * W, (k + 1) * W)
        out[:, span] = held[k]
        out[pl.ds(core_row, HALF), span] += from_core[k]
        out[pl.ds(far_row, HALF), span] += from_far[k]


def copy_all(pairs, sems):
    copies = [
        pltpu.make_async_copy(source, target, sems.at[k])
        for k, (source, target) in enumerate(pairs)
    ]
    for copy in copies:
        copy.start()
    for copy in copies:
        copy.wait()


def gather_body(one, two, three, four, out, sems):
    scan = lax.axis_index("scan")
    parts = enumerate((one, two, three, four))
    copy_all([(part, out.at[lax.rem(scan + 4 - step, 4)]) for step, part in parts], sems)


def halves_body(mine, other, out, sems):
    core = lax.axis_index("core")
    copy_all([(mine, out.at[core]), (other, out.at[1 - core])], sems)


def place_parts(body, shape, parts, name):
    return pl.pallas_call(
        body,
        out_shape=jax.ShapeDtypeStruct(shape, F32),
        in_specs=[ANY] * len(parts),
        out_specs=ANY,
        scratch_shapes=[pltpu.SemaphoreType.DMA((len(parts),))],
        compiler_params=PARAMS,
        cost_estimate=pl.CostEstimate(flops=LONG, bytes_accessed=0, transcendentals=0),
        name=name,
    )(*parts)


def tables():
    index = np.arange(W)
    angle = 2.0 * np.pi * ((index[:, None] * index[None, :]) % W) / W
    cos, sin = np.cos(angle) / np.sqrt(W), -np.sin(angle) / np.sqrt(W)
    right = np.block([[cos, sin], [-sin, cos]])
    arrays = []
    for table in (right, right.T):
        high = table.astype(BF16)
        low = (table - high.astype(np.float64)).astype(BF16)
        arrays += [high, low]
    return [jnp.asarray(a) for a in arrays]


def run_slots(*args):
    message = (2 * W + 8, W)
    share = (MODES * W + 8, W)
    return call(
        slots_body,
        [message] * 4 + [share] * 2,
        (*args, *tables()),
        [SMEM] * 2 + [VMEM] * 16,
        scratch=[
            pltpu.VMEM((4, 3, TILE + 2 * HALF, W), F32),
            pltpu.VMEM((4, 2, W, W), F32),
            pltpu.VMEM((2 * MODES, W, W), F32),
            pltpu.VMEM((4 * MODES, W, W), F32),
            pltpu.VMEM((8, W, W), F32),
        ],
        name="slots",
    )


def per_device(sizes, specimen, probe_modes, kernel_phase, offsets, live_counts, measured):
    nx, ntx, nsc = sizes

    def over_grid(target):
        pairs = []
        for x in range(nx):
            for c in range(2):
                for t in range(ntx):
                    x2, c2, t2 = target(x, c, t)
                    pairs.append(((x * 2 + c) * ntx + t, ((x2 % nx) * 2 + c2) * ntx + t2 % ntx))
        return lambda value: lax.ppermute(value, ("x", "core", "tx"), pairs)

    def across(x, c):
        return x + (1 if c else -1), 1 - c

    to_left = over_grid(lambda x, c, t: (x, c, t - 1))
    to_right = over_grid(lambda x, c, t: (x, c, t + 1))
    to_core = over_grid(lambda x, c, t: (x, 1 - c, t))
    to_far = over_grid(lambda x, c, t: (*across(x, c), t))
    far_left = over_grid(lambda x, c, t: (*across(x, c), t - 1))
    far_right = over_grid(lambda x, c, t: (*across(x, c), t + 1))

    def to_scan(value, step):
        return lax.ppermute(value, "scan", [(s, (s + step) % nsc) for s in range(nsc)])

    def to_pair(value, mask):
        return lax.ppermute(value, "tx", [(t, t ^ mask) for t in range(ntx)])

    tile = specimen.reshape(4, TILE, TILE)
    strip, corner, side = (4, HALF, TILE), (4, HALF // 2, W), (4, W, W)
    left, right = call(sides_body, [side, side], (tile,), [VMEM], name="sides")
    near, far, corner_left, corner_right = call(
        strips_body,
        [strip, strip, corner, corner],
        (tile, left),
        [VMEM, ANY],
        name="strips",
        flops=LONG,
    )
    from_right, from_left = to_left(left), to_right(right)
    from_core, from_far = to_core(near), to_far(far)
    corner_right, corner_left = far_left(corner_left), far_right(corner_right)
    kernel_real, kernel_imag = call(
        phase_body,
        [(W, W)] * 2,
        (kernel_phase, from_right, from_left),
        [VMEM] + [ANY] * 2,
        name="phase",
        flops=LONG,
    )
    (corners,) = call(
        corners_body,
        [(4, HALF, W)],
        (from_right, from_left, from_far, corner_right, corner_left),
        [VMEM] * 2 + [ANY] * 3,
        name="corners",
        flops=LONG,
    )
    corners = to_core(corners)
    rows = jnp.clip(offsets[0, 0, :, 0] + HALF, 0, TILE)
    cols = jnp.clip(offsets[0, 0, :, 1], -HALF, TILE - HALF)
    starts = jnp.stack([rows, jnp.where(cols < 0, cols + 3 * W, cols)], axis=1).reshape(4)
    outs = run_slots(
        starts,
        live_counts,
        tile,
        from_right,
        from_left,
        from_core,
        from_far,
        corner_right,
        corner_left,
        corners,
        probe_modes.reshape(2 * MODES, W, W),
        kernel_real,
        kernel_imag,
        measured[0, 0],
    )
    own, away, probe_send, probe_keep = outs[0], outs[1:4], outs[4], outs[5]
    arrived = [to_scan(value, step) for step, value in enumerate(away, 1)]
    probe_got = to_core(probe_send)
    peers = nx * nsc
    rows = MODES * W // peers
    (chunks,) = call(
        spread_body,
        [(peers, rows + 8, W)],
        (probe_keep, probe_got),
        [VMEM] * 2,
        name="spread",
        flops=LONG,
    )
    chunks = lax.all_to_all(chunks, ("x", "scan"), 0, 0)
    tall = TILE + 2 * HALF
    left, right, held = call(
        place_body,
        [(tall // 2, W)] * 2 + [(3, tall, W)],
        (own, *arrived),
        [VMEM] * 4,
        name="place",
        flops=LONG,
    )
    (share,) = call(
        sum_body, [(rows + 8, W)], (chunks, left), [VMEM, ANY], name="sum", flops=LONG
    )
    left, right = to_left(left), to_right(right)
    group = [share] + [to_pair(share, mask) for mask in range(1, 4)]
    near, far, held = call(
        rows_body,
        [(2, HALF, W)] * 2 + [(2, TILE, W)],
        (right, left, held, share),
        [VMEM] * 3 + [ANY],
        scratch=[pltpu.VMEM((2, tall, W), F32)],
        name="rows",
        flops=LONG,
    )
    (share,) = call(
        group_body, [(rows + 8, W)], (*group, near), [VMEM] * 4 + [ANY], name="group", flops=LONG
    )
    near, far = to_core(near), to_far(far)
    (quarter,) = call(
        finish_body,
        [(TILE, TILE)],
        (near, far, held, share),
        [VMEM] * 3 + [ANY],
        name="finish",
        flops=LONG,
    )
    quarters = [quarter] + [to_scan(quarter, step) for step in range(1, nsc)]
    got = to_pair(share, ntx - 1)
    (spread,) = call(
        mean_body,
        [(peers, rows, W)],
        (share, got),
        [VMEM] * 2,
        name="mean",
        flops=LONG,
    )
    mine = lax.all_to_all(spread, ("x", "scan"), 0, 0).reshape(MODES * W, W)
    other = to_core(mine)
    probe_grad = place_parts(halves_body, (2, MODES * W, W), (mine, other), "halves")
    object_grad = place_parts(gather_body, (4, TILE, TILE), quarters, "gather")
    return object_grad.reshape(specimen.shape), probe_grad.reshape(probe_modes.shape)


def solution(mesh):
    ny, ntx, nsc = mesh.devices.shape
    split = Mesh(mesh.devices.reshape(ny // 2, 2, ntx, nsc), ("x", "core", "tx", "scan"))
    rows = ("x", "core")
    placed = (
        P(None, None, rows, "tx"),
        P(),
        P(),
        P(rows, "tx", "scan", None),
        P(rows, "tx", "scan"),
        P(rows, "tx", "scan", None, None),
    )
    return jax.shard_map(
        functools.partial(per_device, (ny // 2, ntx, nsc)),
        mesh=split,
        in_specs=placed,
        out_specs=(P(None, None, rows, "tx"), P()),
        check_vma=False,
    )
```

```python
import functools

import jax
import jax.numpy as jnp
import numpy as np
from jax import lax
from jax.experimental import pallas as pl
from jax.experimental.pallas import tpu as pltpu
from jax.sharding import Mesh
from jax.sharding import PartitionSpec as P

F32 = jnp.float32
BF16 = jnp.bfloat16
VMEM = pl.BlockSpec(memory_space=pltpu.VMEM)
SMEM = pl.BlockSpec(memory_space=pltpu.SMEM)
ANY = pl.BlockSpec(memory_space=pl.ANY)
LONG = 10**10
CODE = 512
PARAMS = pltpu.CompilerParams(vmem_limit_bytes=48 * 1024 * 1024)
W = 128
HALF = 64
TILE = 256
MODES = 4


def call(body, outs, args, specs, scratch=(), name=None, flops=0):
    return pl.pallas_call(
        body,
        out_shape=[jax.ShapeDtypeStruct(shape, F32) for shape in outs],
        in_specs=specs,
        out_specs=[VMEM] * len(outs),
        scratch_shapes=list(scratch),
        compiler_params=PARAMS,
        cost_estimate=pl.CostEstimate(flops=flops, bytes_accessed=0, transcendentals=0) if flops else None,
        name=name,
    )(*args)


def copy_all(pairs, sems):
    copies = [
        pltpu.make_async_copy(source, target, sems.at[k])
        for k, (source, target) in enumerate(pairs)
    ]
    for copy in copies:
        copy.start()
    for copy in copies:
        copy.wait()


def low_lanes(rows):
    return lax.broadcasted_iota(jnp.int32, (rows, W), 1) < HALF


def swap(x):
    return pltpu.roll(x, HALF, 1)


def rim_rows(core, last):
    return pl.multiple_of((1 - core) * last, HALF), pl.multiple_of(core * last, HALF)


def fold_corner(rows, left, right):
    short = low_lanes(HALF // 2)
    upper, lower = rows[: HALF // 2], rows[HALF // 2 :]
    left[...] = jnp.where(short, upper[:, :W], swap(lower[:, :W]))
    right[...] = jnp.where(short, swap(upper[:, W:]), lower[:, W:])


def sides_body(tile, to_left, to_right):
    wide = low_lanes(W)
    for part in range(4):
        first, second = tile[part, :W, :W], tile[part, W:, :W]
        to_left[part] = jnp.where(wide, first, swap(second))
        first, second = tile[part, :W, W:], tile[part, W:, W:]
        to_right[part] = jnp.where(wide, swap(first), second)


def strips_body(tile, after, to_core, to_far, far_left, far_right):
    core_row, far_row = rim_rows(lax.axis_index("core"), TILE - HALF)
    for part in range(4):
        to_core[part] = tile[part, pl.ds(core_row, HALF), :]
        rows = tile[part, pl.ds(far_row, HALF), :]
        to_far[part] = rows
        fold_corner(rows, far_left.at[part], far_right.at[part])


def corners_body(from_right, from_left, out):
    core = lax.axis_index("core")
    low = low_lanes(HALF)
    span = pl.ds(pl.multiple_of((1 - core) * HALF, HALF), HALF)
    for part in range(4):
        right, left = from_right[part, span], from_left[part, span]
        right = jnp.where(core == 0, swap(right), right)
        left = jnp.where(core == 0, left, swap(left))
        out[part] = jnp.where(low, right, left)


def phase_body(phase, far, right, left, real, imag):
    real[...] = jnp.cos(phase[...])
    imag[...] = jnp.sin(phase[...])


def halves(x):
    high = x.astype(BF16)
    return high, (x - high.astype(F32)).astype(BF16)


def times_right(real, imag, table):
    outs = ([], [])
    for k in range(0, len(real), 2):
        high, low = halves(
            jnp.concatenate(
                [jnp.concatenate([r, i], axis=1) for r, i in zip(real[k : k + 2], imag[k : k + 2])],
                axis=0,
            )
        )
        out = jnp.dot(jnp.concatenate([high, low, high], axis=1), table, preferred_element_type=F32)
        for m in range(2):
            outs[0].append(out[W * m : W * (m + 1), :W])
            outs[1].append(out[W * m : W * (m + 1), W:])
    return outs


def times_left(table, real, imag):
    outs = ([], [])
    for k in range(0, len(real), 2):
        high, low = halves(
            jnp.concatenate(
                [jnp.concatenate(real[k : k + 2], axis=1), jnp.concatenate(imag[k : k + 2], axis=1)],
                axis=0,
            )
        )
        out = jnp.dot(table, jnp.concatenate([high, low, high], axis=0), preferred_element_type=F32)
        for m in range(2):
            outs[0].append(out[:W, W * m : W * (m + 1)])
            outs[1].append(out[W:, W * m : W * (m + 1)])
    return outs


def slots_body(
    starts,
    live_counts,
    tile,
    from_right,
    from_left,
    from_core,
    from_far,
    far_right,
    far_left,
    corners,
    probe,
    kernel_real,
    kernel_imag,
    measured,
    right_high,
    right_low,
    left_high,
    left_low,
    out0,
    out1,
    out2,
    out3,
    probe_send,
    probe_keep,
    wide,
    grads,
    probe_sum,
    mid,
    patches,
):
    core, scan = lax.axis_index("core"), lax.axis_index("scan")
    live = live_counts[0, 0, 0]
    core_row, far_row = rim_rows(core, TILE + HALF)
    tall = low_lanes(W)
    short = low_lanes(HALF // 2)
    for part in range(4):
        wide[part, 0, HALF : HALF + TILE] = tile[part, :, :W]
        wide[part, 1, HALF : HALF + TILE] = tile[part, :, W:]
        right, left = from_right[part], from_left[part]
        wide[part, 2, HALF : HALF + W] = jnp.where(tall, right, swap(left))
        wide[part, 2, HALF + W : HALF + TILE] = jnp.where(tall, swap(right), left)
        for row, strip in ((core_row, from_core), (far_row, from_far)):
            wide[part, 0, pl.ds(row, HALF)] = strip[part, :, :W]
            wide[part, 1, pl.ds(row, HALF)] = strip[part, :, W:]
        wide[part, 2, pl.ds(core_row, HALF)] = corners[part]
        right, left = far_right[part], far_left[part]
        wide[part, 2, pl.ds(far_row, HALF // 2)] = jnp.where(short, right, swap(left))
        lower = pl.multiple_of(far_row + HALF // 2, HALF // 2)
        wide[part, 2, pl.ds(lower, HALF // 2)] = jnp.where(short, swap(right), left)

    def corner(slot):
        return starts[2 * slot], starts[2 * slot + 1]

    forward_right = jnp.concatenate([right_high[...], right_high[...], right_low[...]], axis=0)
    inverse_right = jnp.concatenate([left_high[...], left_high[...], left_low[...]], axis=0)
    forward_left = jnp.concatenate([left_high[...], left_high[...], left_low[...]], axis=1)
    inverse_left = jnp.concatenate([right_high[...], right_high[...], right_low[...]], axis=1)

    def transform(real, imag):
        return times_left(forward_left, *times_right(real, imag, forward_right))

    def untransform(real, imag):
        return times_right(*times_left(inverse_left, real, imag), inverse_right)

    modes = range(MODES)
    lanes = lax.broadcasted_iota(jnp.int32, (W, W), 1)

    for slot in range(2):
        row, col = corner(slot)
        block = col // W
        shift = col - block * W
        after = jnp.where(block == 2, 0, block + 1)
        turn = jnp.where(shift == 0, 0, W - shift)
        for part in range(4):
            one = pltpu.roll(wide[part, block, pl.ds(row, W)], turn, 1)
            two = pltpu.roll(wide[part, after, pl.ds(row, W)], turn, 1)
            patches[4 * slot + part] = jnp.where(lanes < W - shift, one, two)
    slots = range(2)
    pairs = [(slot, m) for slot in slots for m in modes]

    def patch(part):
        return [patches[4 * slot + part] for slot in slots]

    def times(real, imag, by_real, by_imag):
        return (
            [r * by_real[s] - i * by_imag[s] for (s, m), r, i in zip(pairs, real, imag)],
            [r * by_imag[s] + i * by_real[s] for (s, m), r, i in zip(pairs, real, imag)],
        )

    def times_conj(real, imag, by_real, by_imag):
        return (
            [r * by_real[s] + i * by_imag[s] for (s, m), r, i in zip(pairs, real, imag)],
            [i * by_real[s] - r * by_imag[s] for (s, m), r, i in zip(pairs, real, imag)],
        )

    def total(terms):
        return [functools.reduce(jnp.add, terms[MODES * s : MODES * (s + 1)]) for s in slots]

    near_real, near_imag = patch(0), patch(1)
    real, imag = times(
        [probe[2 * m] for s, m in pairs], [probe[2 * m + 1] for s, m in pairs], near_real, near_imag
    )
    real, imag = transform(real, imag)
    kr, ki = [kernel_real[...]] * 2, [kernel_imag[...]] * 2
    real, imag = times(real, imag, kr, ki)
    real, imag = untransform(real, imag)
    for n in range(2 * MODES):
        mid[2 * n] = real[n]
        mid[2 * n + 1] = imag[n]
    away_real, away_imag = patch(2), patch(3)
    real, imag = times(real, imag, away_real, away_imag)
    real, imag = transform(real, imag)
    intensity = total([r * r + i * i for r, i in zip(real, imag)])
    residual = [
        (intensity[s] - measured[s]) * jnp.where(s < live, 2.0, 0.0).astype(F32) for s in slots
    ]
    real = [r * residual[s] for (s, m), r in zip(pairs, real)]
    imag = [i * residual[s] for (s, m), i in zip(pairs, imag)]
    real, imag = untransform(real, imag)
    both = range(2 * MODES)
    grad_real = total([mid[2 * n] * real[n] + mid[2 * n + 1] * imag[n] for n in both])
    grad_imag = total([mid[2 * n] * imag[n] - mid[2 * n + 1] * real[n] for n in both])
    for s in slots:
        grads[2, s] = grad_real[s]
        grads[3, s] = grad_imag[s]
    real, imag = times_conj(real, imag, patch(2), patch(3))
    real, imag = transform(real, imag)
    real, imag = times_conj(real, imag, kr, ki)
    real, imag = untransform(real, imag)
    grad_real = total([probe[2 * m] * real[n] + probe[2 * m + 1] * imag[n] for n, (s, m) in enumerate(pairs)])
    grad_imag = total([probe[2 * m] * imag[n] - probe[2 * m + 1] * real[n] for n, (s, m) in enumerate(pairs)])
    for s in slots:
        grads[0, s] = grad_real[s]
        grads[1, s] = grad_imag[s]
    real, imag = times_conj(real, imag, patch(0), patch(1))
    for m in modes:
        probe_sum[2 * m] = real[m] + real[MODES + m]
        probe_sum[2 * m + 1] = imag[m] + imag[MODES + m]

    places = lax.broadcasted_iota(jnp.int32, (8, W), 0)
    marks = jnp.zeros((8, W), F32)
    for slot in range(2):
        row, col = corner(slot)
        marks = jnp.where(places == slot, (row * CODE + col).astype(F32), marks)
    for step, out in enumerate((out0, out1, out2, out3)):
        part = lax.rem(scan + step, 4)
        for slot in range(2):
            out[W * slot : W * (slot + 1)] = grads[part, slot]
        out[2 * W :] = marks
    count = jnp.zeros((8, W), F32) + live.astype(F32)
    for half, out in ((core, probe_keep), (1 - core, probe_send)):
        for k in range(MODES):
            out[W * k : W * (k + 1)] = probe_sum[half * MODES + k]
        out[MODES * W :] = count


def spread_body(keep, got, out):
    rows = out.shape[1] - 8
    count = keep[MODES * W :] + got[MODES * W :]
    for k in range(out.shape[0]):
        span = slice(k * rows, (k + 1) * rows)
        out[k, :rows] = keep[span] + got[span]
        out[k, rows:] = count


def sum_body(chunks, after, out):
    out[...] = functools.reduce(jnp.add, [chunks[k] for k in range(chunks.shape[0])])


def pair_body(own, got, after, out):
    out[...] = own[...] + got[...]


def mean_body(own, got, spread):
    total = own[...] + got[...]
    rows = spread.shape[1]
    mean = total[:rows] / total[rows : rows + 1]
    for k in range(spread.shape[0]):
        spread[k] = mean


def place_body(one, two, three, four, to_left, to_right, wide):
    messages = (one, two, three, four)
    spots = []
    for message in messages:
        for slot in range(2):
            code = jnp.max(message[2 * W + slot : 2 * W + slot + 1]).astype(jnp.int32)
            row, col = code // CODE, lax.rem(code, CODE)
            row = jnp.clip(row, 0, TILE)
            col = jnp.clip(col, 0, 3 * W - 1)
            block = col // W
            after = jnp.where(block == 2, 0, block + 1)
            spots.append((row, block, after, col - block * W))
    wide[...] = jnp.zeros_like(wide)
    lanes = lax.broadcasted_iota(jnp.int32, (W, W), 1)
    for k, message in enumerate(messages):
        for slot in range(2):
            row, block, after, shift = spots[2 * k + slot]
            turned = pltpu.roll(message[W * slot : W * (slot + 1)], shift, 1)
            wide[block, pl.ds(row, W)] += jnp.where(lanes >= shift, turned, 0.0)
            wide[after, pl.ds(row, W)] += jnp.where(lanes < shift, turned, 0.0)
    half = (TILE + 2 * HALF) // 2
    low = low_lanes(half)
    upper, lower = wide[2, :half], wide[2, half:]
    to_right[...] = jnp.where(low, upper, swap(lower))
    to_left[...] = jnp.where(low, swap(upper), lower)


def rows_body(from_left, from_right, held, after, to_core, to_far, keep, wide):
    half = (TILE + 2 * HALF) // 2
    low = low_lanes(half)
    left, right = from_left[...], from_right[...]
    wide[0, :half] = held[0, :half] + jnp.where(low, left, 0.0)
    wide[0, half:] = held[0, half:] + jnp.where(low, swap(left), 0.0)
    wide[1, :half] = held[1, :half] + jnp.where(low, 0.0, swap(right))
    wide[1, half:] = held[1, half:] + jnp.where(low, 0.0, right)
    core_row, far_row = rim_rows(lax.axis_index("core"), TILE + HALF)
    for k in range(2):
        to_core[k] = wide[k, pl.ds(core_row, HALF)]
        to_far[k] = wide[k, pl.ds(far_row, HALF)]
        keep[k] = wide[k, HALF : HALF + TILE]


def finish_body(from_core, from_far, held, after, out):
    core_row, far_row = rim_rows(lax.axis_index("core"), TILE - HALF)
    for k in range(2):
        span = slice(k * W, (k + 1) * W)
        out[:, span] = held[k]
        out[pl.ds(core_row, HALF), span] += from_core[k]
        out[pl.ds(far_row, HALF), span] += from_far[k]


def gather_body(one, two, three, four, out, sems):
    scan = lax.axis_index("scan")
    parts = enumerate((one, two, three, four))
    copy_all([(part, out.at[lax.rem(scan + 4 - step, 4)]) for step, part in parts], sems)


def halves_body(mine, other, out, sems):
    core = lax.axis_index("core")
    copy_all([(mine, out.at[core]), (other, out.at[1 - core])], sems)


def place_parts(body, shape, parts, name):
    return pl.pallas_call(
        body,
        out_shape=jax.ShapeDtypeStruct(shape, F32),
        in_specs=[ANY] * len(parts),
        out_specs=ANY,
        scratch_shapes=[pltpu.SemaphoreType.DMA((len(parts),))],
        compiler_params=PARAMS,
        cost_estimate=pl.CostEstimate(flops=LONG, bytes_accessed=0, transcendentals=0),
        name=name,
    )(*parts)


def tables():
    index = np.arange(W)
    angle = 2.0 * np.pi * ((index[:, None] * index[None, :]) % W) / W
    cos, sin = np.cos(angle) / np.sqrt(W), -np.sin(angle) / np.sqrt(W)
    right = np.block([[cos, sin], [-sin, cos]])
    arrays = []
    for table in (right, right.T):
        high = table.astype(BF16)
        low = (table - high.astype(np.float64)).astype(BF16)
        arrays += [high, low]
    return [jnp.asarray(a) for a in arrays]


def run_slots(*args):
    message = (2 * W + 8, W)
    share = (MODES * W + 8, W)
    return call(
        slots_body,
        [message] * 4 + [share] * 2,
        (*args, *tables()),
        [SMEM] * 2 + [VMEM] * 16,
        scratch=[
            pltpu.VMEM((4, 3, TILE + 2 * HALF, W), F32),
            pltpu.VMEM((4, 2, W, W), F32),
            pltpu.VMEM((2 * MODES, W, W), F32),
            pltpu.VMEM((4 * MODES, W, W), F32),
            pltpu.VMEM((8, W, W), F32),
        ],
        name="slots",
    )


def per_device(sizes, specimen, probe_modes, kernel_phase, offsets, live_counts, measured):
    nx, ntx, nsc = sizes

    def over_grid(target):
        pairs = []
        for x in range(nx):
            for c in range(2):
                for t in range(ntx):
                    x2, c2, t2 = target(x, c, t)
                    pairs.append(((x * 2 + c) * ntx + t, ((x2 % nx) * 2 + c2) * ntx + t2 % ntx))
        return lambda value: lax.ppermute(value, ("x", "core", "tx"), pairs)

    def across(x, c):
        return x + (1 if c else -1), 1 - c

    to_left = over_grid(lambda x, c, t: (x, c, t - 1))
    to_right = over_grid(lambda x, c, t: (x, c, t + 1))
    to_core = over_grid(lambda x, c, t: (x, 1 - c, t))
    to_far = over_grid(lambda x, c, t: (*across(x, c), t))
    far_left = over_grid(lambda x, c, t: (*across(x, c), t - 1))
    far_right = over_grid(lambda x, c, t: (*across(x, c), t + 1))

    def to_scan(value, step):
        return lax.ppermute(value, "scan", [(s, (s + step) % nsc) for s in range(nsc)])

    def to_pair(value, mask):
        return lax.ppermute(value, "tx", [(t, t ^ mask) for t in range(ntx)])

    tile = specimen.reshape(4, TILE, TILE)
    strip, corner, side = (4, HALF, TILE), (4, HALF // 2, W), (4, W, W)
    left, right = call(sides_body, [side, side], (tile,), [VMEM], name="sides")
    near, far, corner_left, corner_right = call(
        strips_body,
        [strip, strip, corner, corner],
        (tile, left),
        [VMEM, ANY],
        name="strips",
        flops=LONG,
    )
    from_right, from_left = to_left(left), to_right(right)
    from_core, from_far = to_core(near), to_far(far)
    corner_right, corner_left = far_left(corner_left), far_right(corner_right)
    (corners,) = call(
        corners_body, [(4, HALF, W)], (from_right, from_left), [VMEM] * 2, name="corners"
    )
    corners = to_core(corners)
    kernel_real, kernel_imag = call(
        phase_body,
        [(W, W)] * 2,
        (kernel_phase, from_far, corner_right, corner_left),
        [VMEM] + [ANY] * 3,
        name="phase",
        flops=LONG,
    )
    rows = jnp.clip(offsets[0, 0, :, 0] + HALF, 0, TILE)
    cols = jnp.clip(offsets[0, 0, :, 1], -HALF, TILE - HALF)
    starts = jnp.stack([rows, jnp.where(cols < 0, cols + 3 * W, cols)], axis=1).reshape(4)
    outs = run_slots(
        starts,
        live_counts,
        tile,
        from_right,
        from_left,
        from_core,
        from_far,
        corner_right,
        corner_left,
        corners,
        probe_modes.reshape(2 * MODES, W, W),
        kernel_real,
        kernel_imag,
        measured[0, 0],
    )
    own, away, probe_send, probe_keep = outs[0], outs[1:4], outs[4], outs[5]
    arrived = [to_scan(value, step) for step, value in enumerate(away, 1)]
    probe_got = to_core(probe_send)
    peers = nx * nsc
    rows = MODES * W // peers
    (chunks,) = call(
        spread_body,
        [(peers, rows + 8, W)],
        (probe_keep, probe_got),
        [VMEM] * 2,
        name="spread",
        flops=LONG,
    )
    chunks = lax.all_to_all(chunks, ("x", "scan"), 0, 0)
    tall = TILE + 2 * HALF
    left, right, held = call(
        place_body,
        [(tall // 2, W)] * 2 + [(3, tall, W)],
        (own, *arrived),
        [VMEM] * 4,
        name="place",
        flops=LONG,
    )
    (share,) = call(
        sum_body, [(rows + 8, W)], (chunks, left), [VMEM, ANY], name="sum", flops=LONG
    )
    left, right = to_left(left), to_right(right)
    got = to_pair(share, 1)
    near, far, held = call(
        rows_body,
        [(2, HALF, W)] * 2 + [(2, TILE, W)],
        (right, left, held, share),
        [VMEM] * 3 + [ANY],
        scratch=[pltpu.VMEM((2, tall, W), F32)],
        name="rows",
        flops=LONG,
    )
    (share,) = call(
        pair_body, [(rows + 8, W)], (share, got, near), [VMEM] * 2 + [ANY], name="pair", flops=LONG
    )
    got = to_pair(share, 2)
    near, far = to_core(near), to_far(far)
    (quarter,) = call(
        finish_body,
        [(TILE, TILE)],
        (near, far, held, share),
        [VMEM] * 3 + [ANY],
        name="finish",
        flops=LONG,
    )
    quarters = [quarter] + [to_scan(quarter, step) for step in range(1, nsc)]
    (share,) = call(
        pair_body, [(rows + 8, W)], (share, got, quarter), [VMEM] * 2 + [ANY], name="pair", flops=LONG
    )
    got = to_pair(share, ntx - 1)
    (spread,) = call(
        mean_body,
        [(peers, rows, W)],
        (share, got),
        [VMEM] * 2,
        name="mean",
        flops=LONG,
    )
    mine = lax.all_to_all(spread, ("x", "scan"), 0, 0).reshape(MODES * W, W)
    other = to_core(mine)
    probe_grad = place_parts(halves_body, (2, MODES * W, W), (mine, other), "halves")
    object_grad = place_parts(gather_body, (4, TILE, TILE), quarters, "gather")
    return object_grad.reshape(specimen.shape), probe_grad.reshape(probe_modes.shape)


def solution(mesh):
    ny, ntx, nsc = mesh.devices.shape
    split = Mesh(mesh.devices.reshape(ny // 2, 2, ntx, nsc), ("x", "core", "tx", "scan"))
    rows = ("x", "core")
    placed = (
        P(None, None, rows, "tx"),
        P(),
        P(),
        P(rows, "tx", "scan", None),
        P(rows, "tx", "scan"),
        P(rows, "tx", "scan", None, None),
    )
    return jax.shard_map(
        functools.partial(per_device, (ny // 2, ntx, nsc)),
        mesh=split,
        in_specs=placed,
        out_specs=(P(None, None, rows, "tx"), P()),
        check_vma=False,
    )
```

```python
import functools

import jax
import jax.numpy as jnp
import numpy as np
from jax import lax
from jax.experimental import pallas as pl
from jax.experimental.pallas import tpu as pltpu
from jax.sharding import Mesh
from jax.sharding import PartitionSpec as P

F32 = jnp.float32
BF16 = jnp.bfloat16
VMEM = pl.BlockSpec(memory_space=pltpu.VMEM)
SMEM = pl.BlockSpec(memory_space=pltpu.SMEM)
ANY = pl.BlockSpec(memory_space=pl.ANY)
LONG = 10**10
CODE = 512
PARAMS = pltpu.CompilerParams(vmem_limit_bytes=48 * 1024 * 1024)
W = 128
HALF = 64
TILE = 256
MODES = 4


def call(body, outs, args, specs, scratch=(), name=None, flops=0):
    return pl.pallas_call(
        body,
        out_shape=[jax.ShapeDtypeStruct(shape, F32) for shape in outs],
        in_specs=specs,
        out_specs=[VMEM] * len(outs),
        scratch_shapes=list(scratch),
        compiler_params=PARAMS,
        cost_estimate=pl.CostEstimate(flops=flops, bytes_accessed=0, transcendentals=0) if flops else None,
        name=name,
    )(*args)


def copy_all(pairs, sems):
    copies = [
        pltpu.make_async_copy(source, target, sems.at[k])
        for k, (source, target) in enumerate(pairs)
    ]
    for copy in copies:
        copy.start()
    for copy in copies:
        copy.wait()


def low_lanes(rows):
    return lax.broadcasted_iota(jnp.int32, (rows, W), 1) < HALF


def swap(x):
    return pltpu.roll(x, HALF, 1)


def rim_rows(core, last):
    return pl.multiple_of((1 - core) * last, HALF), pl.multiple_of(core * last, HALF)


def fold_corner(rows, left, right):
    short = low_lanes(HALF // 2)
    upper, lower = rows[: HALF // 2], rows[HALF // 2 :]
    left[...] = jnp.where(short, upper[:, :W], swap(lower[:, :W]))
    right[...] = jnp.where(short, swap(upper[:, W:]), lower[:, W:])


def right_body(tile, to_right):
    wide = low_lanes(W)
    for part in range(4):
        first, second = tile[part, :W, W:], tile[part, W:, W:]
        to_right[part] = jnp.where(wide, swap(first), second)


def left_body(tile, after, to_left):
    wide = low_lanes(W)
    for part in range(4):
        first, second = tile[part, :W, :W], tile[part, W:, :W]
        to_left[part] = jnp.where(wide, first, swap(second))


def strips_body(tile, after, to_core, to_far, far_left, far_right):
    core_row, far_row = rim_rows(lax.axis_index("core"), TILE - HALF)
    for part in range(4):
        to_core[part] = tile[part, pl.ds(core_row, HALF), :]
        rows = tile[part, pl.ds(far_row, HALF), :]
        to_far[part] = rows
        fold_corner(rows, far_left.at[part], far_right.at[part])


def corners_body(from_right, from_left, out):
    core = lax.axis_index("core")
    low = low_lanes(HALF)
    span = pl.ds(pl.multiple_of((1 - core) * HALF, HALF), HALF)
    for part in range(4):
        right, left = from_right[part, span], from_left[part, span]
        right = jnp.where(core == 0, swap(right), right)
        left = jnp.where(core == 0, left, swap(left))
        out[part] = jnp.where(low, right, left)


def guard_body(far, right, left, mark):
    mark[...] = jnp.zeros_like(mark)


def phase_body(phase, real, imag):
    real[...] = jnp.cos(phase[...])
    imag[...] = jnp.sin(phase[...])


def halves(x):
    high = x.astype(BF16)
    return high, (x - high.astype(F32)).astype(BF16)


def times_right(real, imag, table):
    outs = ([], [])
    for k in range(0, len(real), 2):
        high, low = halves(
            jnp.concatenate(
                [jnp.concatenate([r, i], axis=1) for r, i in zip(real[k : k + 2], imag[k : k + 2])],
                axis=0,
            )
        )
        out = jnp.dot(jnp.concatenate([high, low, high], axis=1), table, preferred_element_type=F32)
        for m in range(2):
            outs[0].append(out[W * m : W * (m + 1), :W])
            outs[1].append(out[W * m : W * (m + 1), W:])
    return outs


def times_left(table, real, imag):
    outs = ([], [])
    for k in range(0, len(real), 2):
        high, low = halves(
            jnp.concatenate(
                [jnp.concatenate(real[k : k + 2], axis=1), jnp.concatenate(imag[k : k + 2], axis=1)],
                axis=0,
            )
        )
        out = jnp.dot(table, jnp.concatenate([high, low, high], axis=0), preferred_element_type=F32)
        for m in range(2):
            outs[0].append(out[:W, W * m : W * (m + 1)])
            outs[1].append(out[W:, W * m : W * (m + 1)])
    return outs


def slots_body(
    starts,
    live_counts,
    tile,
    from_right,
    from_left,
    from_core,
    from_far,
    far_right,
    far_left,
    corners,
    mark,
    probe,
    kernel_real,
    kernel_imag,
    measured,
    right_high,
    right_low,
    left_high,
    left_low,
    out0,
    out1,
    out2,
    out3,
    probe_send,
    probe_keep,
    wide,
    grads,
    probe_sum,
    mid,
    patches,
):
    core, scan = lax.axis_index("core"), lax.axis_index("scan")
    live = live_counts[0, 0, 0]
    core_row, far_row = rim_rows(core, TILE + HALF)
    tall = low_lanes(W)
    short = low_lanes(HALF // 2)
    for part in range(4):
        wide[part, 0, HALF : HALF + TILE] = tile[part, :, :W]
        wide[part, 1, HALF : HALF + TILE] = tile[part, :, W:]
        right, left = from_right[part], from_left[part]
        wide[part, 2, HALF : HALF + W] = jnp.where(tall, right, swap(left))
        wide[part, 2, HALF + W : HALF + TILE] = jnp.where(tall, swap(right), left)
        for row, strip in ((core_row, from_core), (far_row, from_far)):
            wide[part, 0, pl.ds(row, HALF)] = strip[part, :, :W]
            wide[part, 1, pl.ds(row, HALF)] = strip[part, :, W:]
        wide[part, 2, pl.ds(core_row, HALF)] = corners[part]
        right, left = far_right[part], far_left[part]
        wide[part, 2, pl.ds(far_row, HALF // 2)] = jnp.where(short, right, swap(left))
        lower = pl.multiple_of(far_row + HALF // 2, HALF // 2)
        wide[part, 2, pl.ds(lower, HALF // 2)] = jnp.where(short, swap(right), left)

    def corner(slot):
        return starts[2 * slot], starts[2 * slot + 1]

    forward_right = jnp.concatenate([right_high[...], right_high[...], right_low[...]], axis=0)
    inverse_right = jnp.concatenate([left_high[...], left_high[...], left_low[...]], axis=0)
    forward_left = jnp.concatenate([left_high[...], left_high[...], left_low[...]], axis=1)
    inverse_left = jnp.concatenate([right_high[...], right_high[...], right_low[...]], axis=1)

    def transform(real, imag):
        return times_left(forward_left, *times_right(real, imag, forward_right))

    def untransform(real, imag):
        return times_right(*times_left(inverse_left, real, imag), inverse_right)

    modes = range(MODES)
    lanes = lax.broadcasted_iota(jnp.int32, (W, W), 1)

    for slot in range(2):
        row, col = corner(slot)
        block = col // W
        shift = col - block * W
        after = jnp.where(block == 2, 0, block + 1)
        turn = jnp.where(shift == 0, 0, W - shift)
        for part in range(4):
            one = pltpu.roll(wide[part, block, pl.ds(row, W)], turn, 1)
            two = pltpu.roll(wide[part, after, pl.ds(row, W)], turn, 1)
            patches[4 * slot + part] = jnp.where(lanes < W - shift, one, two)
    slots = range(2)
    pairs = [(slot, m) for slot in slots for m in modes]

    def patch(part):
        return [patches[4 * slot + part] for slot in slots]

    def times(real, imag, by_real, by_imag):
        return (
            [r * by_real[s] - i * by_imag[s] for (s, m), r, i in zip(pairs, real, imag)],
            [r * by_imag[s] + i * by_real[s] for (s, m), r, i in zip(pairs, real, imag)],
        )

    def times_conj(real, imag, by_real, by_imag):
        return (
            [r * by_real[s] + i * by_imag[s] for (s, m), r, i in zip(pairs, real, imag)],
            [i * by_real[s] - r * by_imag[s] for (s, m), r, i in zip(pairs, real, imag)],
        )

    def total(terms):
        return [functools.reduce(jnp.add, terms[MODES * s : MODES * (s + 1)]) for s in slots]

    near_real, near_imag = patch(0), patch(1)
    real, imag = times(
        [probe[2 * m] for s, m in pairs], [probe[2 * m + 1] for s, m in pairs], near_real, near_imag
    )
    real, imag = transform(real, imag)
    kr, ki = [kernel_real[...]] * 2, [kernel_imag[...]] * 2
    real, imag = times(real, imag, kr, ki)
    real, imag = untransform(real, imag)
    for n in range(2 * MODES):
        mid[2 * n] = real[n]
        mid[2 * n + 1] = imag[n]
    away_real, away_imag = patch(2), patch(3)
    real, imag = times(real, imag, away_real, away_imag)
    real, imag = transform(real, imag)
    intensity = total([r * r + i * i for r, i in zip(real, imag)])
    residual = [
        (intensity[s] - measured[s]) * jnp.where(s < live, 2.0, 0.0).astype(F32) for s in slots
    ]
    real = [r * residual[s] for (s, m), r in zip(pairs, real)]
    imag = [i * residual[s] for (s, m), i in zip(pairs, imag)]
    real, imag = untransform(real, imag)
    both = range(2 * MODES)
    grad_real = total([mid[2 * n] * real[n] + mid[2 * n + 1] * imag[n] for n in both])
    grad_imag = total([mid[2 * n] * imag[n] - mid[2 * n + 1] * real[n] for n in both])
    for s in slots:
        grads[2, s] = grad_real[s]
        grads[3, s] = grad_imag[s]
    real, imag = times_conj(real, imag, patch(2), patch(3))
    real, imag = transform(real, imag)
    real, imag = times_conj(real, imag, kr, ki)
    real, imag = untransform(real, imag)
    grad_real = total([probe[2 * m] * real[n] + probe[2 * m + 1] * imag[n] for n, (s, m) in enumerate(pairs)])
    grad_imag = total([probe[2 * m] * imag[n] - probe[2 * m + 1] * real[n] for n, (s, m) in enumerate(pairs)])
    for s in slots:
        grads[0, s] = grad_real[s]
        grads[1, s] = grad_imag[s]
    real, imag = times_conj(real, imag, patch(0), patch(1))
    for m in modes:
        probe_sum[2 * m] = real[m] + real[MODES + m]
        probe_sum[2 * m + 1] = imag[m] + imag[MODES + m]

    places = lax.broadcasted_iota(jnp.int32, (8, W), 0)
    marks = jnp.zeros((8, W), F32)
    for slot in range(2):
        row, col = corner(slot)
        marks = jnp.where(places == slot, (row * CODE + col).astype(F32), marks)
    for step, out in enumerate((out0, out1, out2, out3)):
        part = lax.rem(scan + step, 4)
        for slot in range(2):
            out[W * slot : W * (slot + 1)] = grads[part, slot]
        out[2 * W :] = marks
    count = jnp.zeros((8, W), F32) + live.astype(F32)
    for half, out in ((core, probe_keep), (1 - core, probe_send)):
        for k in range(MODES):
            out[W * k : W * (k + 1)] = probe_sum[half * MODES + k]
        out[MODES * W :] = count


def spread_body(keep, got, out):
    rows = out.shape[1] - 8
    count = keep[MODES * W :] + got[MODES * W :]
    for k in range(out.shape[0]):
        span = slice(k * rows, (k + 1) * rows)
        out[k, :rows] = keep[span] + got[span]
        out[k, rows:] = count


def sum_body(chunks, after, out):
    out[...] = functools.reduce(jnp.add, [chunks[k] for k in range(chunks.shape[0])])


def pair_body(own, got, after, out):
    out[...] = own[...] + got[...]


def mean_body(own, got, spread):
    total = own[...] + got[...]
    rows = spread.shape[1]
    mean = total[:rows] / total[rows : rows + 1]
    for k in range(spread.shape[0]):
        spread[k] = mean


def place_body(one, two, three, four, to_left, to_right, wide):
    messages = (one, two, three, four)
    spots = []
    for message in messages:
        for slot in range(2):
            code = jnp.max(message[2 * W + slot : 2 * W + slot + 1]).astype(jnp.int32)
            row, col = code // CODE, lax.rem(code, CODE)
            row = jnp.clip(row, 0, TILE)
            col = jnp.clip(col, 0, 3 * W - 1)
            block = col // W
            after = jnp.where(block == 2, 0, block + 1)
            spots.append((row, block, after, col - block * W))
    wide[...] = jnp.zeros_like(wide)
    lanes = lax.broadcasted_iota(jnp.int32, (W, W), 1)
    for k, message in enumerate(messages):
        for slot in range(2):
            row, block, after, shift = spots[2 * k + slot]
            turned = pltpu.roll(message[W * slot : W * (slot + 1)], shift, 1)
            wide[block, pl.ds(row, W)] += jnp.where(lanes >= shift, turned, 0.0)
            wide[after, pl.ds(row, W)] += jnp.where(lanes < shift, turned, 0.0)
    half = (TILE + 2 * HALF) // 2
    low = low_lanes(half)
    upper, lower = wide[2, :half], wide[2, half:]
    to_right[...] = jnp.where(low, upper, swap(lower))
    to_left[...] = jnp.where(low, swap(upper), lower)


def rows_body(from_left, from_right, held, after, to_core, to_far, keep, wide):
    half = (TILE + 2 * HALF) // 2
    low = low_lanes(half)
    left, right = from_left[...], from_right[...]
    wide[0, :half] = held[0, :half] + jnp.where(low, left, 0.0)
    wide[0, half:] = held[0, half:] + jnp.where(low, swap(left), 0.0)
    wide[1, :half] = held[1, :half] + jnp.where(low, 0.0, swap(right))
    wide[1, half:] = held[1, half:] + jnp.where(low, 0.0, right)
    core_row, far_row = rim_rows(lax.axis_index("core"), TILE + HALF)
    for k in range(2):
        to_core[k] = wide[k, pl.ds(core_row, HALF)]
        to_far[k] = wide[k, pl.ds(far_row, HALF)]
        keep[k] = wide[k, HALF : HALF + TILE]


def finish_body(from_core, from_far, held, after, out):
    core_row, far_row = rim_rows(lax.axis_index("core"), TILE - HALF)
    for k in range(2):
        span = slice(k * W, (k + 1) * W)
        out[:, span] = held[k]
        out[pl.ds(core_row, HALF), span] += from_core[k]
        out[pl.ds(far_row, HALF), span] += from_far[k]


def gather_body(one, two, three, four, out, sems):
    scan = lax.axis_index("scan")
    parts = enumerate((one, two, three, four))
    copy_all([(part, out.at[lax.rem(scan + 4 - step, 4)]) for step, part in parts], sems)


def halves_body(mine, other, out, sems):
    core = lax.axis_index("core")
    copy_all([(mine, out.at[core]), (other, out.at[1 - core])], sems)


def place_parts(body, shape, parts, name):
    return pl.pallas_call(
        body,
        out_shape=jax.ShapeDtypeStruct(shape, F32),
        in_specs=[ANY] * len(parts),
        out_specs=ANY,
        scratch_shapes=[pltpu.SemaphoreType.DMA((len(parts),))],
        compiler_params=PARAMS,
        cost_estimate=pl.CostEstimate(flops=LONG, bytes_accessed=0, transcendentals=0),
        name=name,
    )(*parts)


def tables():
    index = np.arange(W)
    angle = 2.0 * np.pi * ((index[:, None] * index[None, :]) % W) / W
    cos, sin = np.cos(angle) / np.sqrt(W), -np.sin(angle) / np.sqrt(W)
    right = np.block([[cos, sin], [-sin, cos]])
    arrays = []
    for table in (right, right.T):
        high = table.astype(BF16)
        low = (table - high.astype(np.float64)).astype(BF16)
        arrays += [high, low]
    return [jnp.asarray(a) for a in arrays]


def run_slots(*args):
    message = (2 * W + 8, W)
    share = (MODES * W + 8, W)
    return call(
        slots_body,
        [message] * 4 + [share] * 2,
        (*args, *tables()),
        [SMEM] * 2 + [VMEM] * 8 + [ANY] + [VMEM] * 8,
        scratch=[
            pltpu.VMEM((4, 3, TILE + 2 * HALF, W), F32),
            pltpu.VMEM((4, 2, W, W), F32),
            pltpu.VMEM((2 * MODES, W, W), F32),
            pltpu.VMEM((4 * MODES, W, W), F32),
            pltpu.VMEM((8, W, W), F32),
        ],
        name="slots",
    )


def per_device(sizes, specimen, probe_modes, kernel_phase, offsets, live_counts, measured):
    nx, ntx, nsc = sizes

    def over_grid(target):
        pairs = []
        for x in range(nx):
            for c in range(2):
                for t in range(ntx):
                    x2, c2, t2 = target(x, c, t)
                    pairs.append(((x * 2 + c) * ntx + t, ((x2 % nx) * 2 + c2) * ntx + t2 % ntx))
        return lambda value: lax.ppermute(value, ("x", "core", "tx"), pairs)

    def across(x, c):
        return x + (1 if c else -1), 1 - c

    to_left = over_grid(lambda x, c, t: (x, c, t - 1))
    to_right = over_grid(lambda x, c, t: (x, c, t + 1))
    to_core = over_grid(lambda x, c, t: (x, 1 - c, t))
    to_far = over_grid(lambda x, c, t: (*across(x, c), t))
    far_left = over_grid(lambda x, c, t: (*across(x, c), t - 1))
    far_right = over_grid(lambda x, c, t: (*across(x, c), t + 1))

    def to_scan(value, step):
        return lax.ppermute(value, "scan", [(s, (s + step) % nsc) for s in range(nsc)])

    def to_pair(value, mask):
        return lax.ppermute(value, "tx", [(t, t ^ mask) for t in range(ntx)])

    tile = specimen.reshape(4, TILE, TILE)
    strip, corner, side = (4, HALF, TILE), (4, HALF // 2, W), (4, W, W)
    (right,) = call(right_body, [side], (tile,), [VMEM], name="right")
    (left,) = call(left_body, [side], (tile, right), [VMEM, ANY], name="left", flops=LONG)
    near, far, corner_left, corner_right = call(
        strips_body,
        [strip, strip, corner, corner],
        (tile, left),
        [VMEM, ANY],
        name="strips",
        flops=LONG,
    )
    from_right, from_left = to_left(left), to_right(right)
    from_core, from_far = to_core(near), to_far(far)
    corner_right, corner_left = far_left(corner_left), far_right(corner_right)
    (corners,) = call(
        corners_body, [(4, HALF, W)], (from_right, from_left), [VMEM] * 2, name="corners"
    )
    corners = to_core(corners)
    (mark,) = call(
        guard_body,
        [(8, W)],
        (from_far, corner_right, corner_left),
        [ANY] * 3,
        name="guard",
        flops=LONG,
    )
    kernel_real, kernel_imag = call(
        phase_body, [(W, W)] * 2, (kernel_phase,), [VMEM], name="phase"
    )
    rows = jnp.clip(offsets[0, 0, :, 0] + HALF, 0, TILE)
    cols = jnp.clip(offsets[0, 0, :, 1], -HALF, TILE - HALF)
    starts = jnp.stack([rows, jnp.where(cols < 0, cols + 3 * W, cols)], axis=1).reshape(4)
    outs = run_slots(
        starts,
        live_counts,
        tile,
        from_right,
        from_left,
        from_core,
        from_far,
        corner_right,
        corner_left,
        corners,
        mark,
        probe_modes.reshape(2 * MODES, W, W),
        kernel_real,
        kernel_imag,
        measured[0, 0],
    )
    own, away, probe_send, probe_keep = outs[0], outs[1:4], outs[4], outs[5]
    arrived = [to_scan(value, step) for step, value in enumerate(away, 1)]
    probe_got = to_core(probe_send)
    peers = nx * nsc
    rows = MODES * W // peers
    (chunks,) = call(
        spread_body,
        [(peers, rows + 8, W)],
        (probe_keep, probe_got),
        [VMEM] * 2,
        name="spread",
        flops=LONG,
    )
    chunks = lax.all_to_all(chunks, ("x", "scan"), 0, 0)
    tall = TILE + 2 * HALF
    left, right, held = call(
        place_body,
        [(tall // 2, W)] * 2 + [(3, tall, W)],
        (own, *arrived),
        [VMEM] * 4,
        name="place",
        flops=LONG,
    )
    (share,) = call(
        sum_body, [(rows + 8, W)], (chunks, left), [VMEM, ANY], name="sum", flops=LONG
    )
    left, right = to_left(left), to_right(right)
    got = to_pair(share, 1)
    near, far, held = call(
        rows_body,
        [(2, HALF, W)] * 2 + [(2, TILE, W)],
        (right, left, held, share),
        [VMEM] * 3 + [ANY],
        scratch=[pltpu.VMEM((2, tall, W), F32)],
        name="rows",
        flops=LONG,
    )
    (share,) = call(
        pair_body, [(rows + 8, W)], (share, got, near), [VMEM] * 2 + [ANY], name="pair", flops=LONG
    )
    got = to_pair(share, 2)
    near, far = to_core(near), to_far(far)
    (quarter,) = call(
        finish_body,
        [(TILE, TILE)],
        (near, far, held, share),
        [VMEM] * 3 + [ANY],
        name="finish",
        flops=LONG,
    )
    quarters = [quarter] + [to_scan(quarter, step) for step in range(1, nsc)]
    (share,) = call(
        pair_body, [(rows + 8, W)], (share, got, quarter), [VMEM] * 2 + [ANY], name="pair", flops=LONG
    )
    got = to_pair(share, ntx - 1)
    (spread,) = call(
        mean_body,
        [(peers, rows, W)],
        (share, got),
        [VMEM] * 2,
        name="mean",
        flops=LONG,
    )
    mine = lax.all_to_all(spread, ("x", "scan"), 0, 0).reshape(MODES * W, W)
    other = to_core(mine)
    probe_grad = place_parts(halves_body, (2, MODES * W, W), (mine, other), "halves")
    object_grad = place_parts(gather_body, (4, TILE, TILE), quarters, "gather")
    return object_grad.reshape(specimen.shape), probe_grad.reshape(probe_modes.shape)


def solution(mesh):
    ny, ntx, nsc = mesh.devices.shape
    split = Mesh(mesh.devices.reshape(ny // 2, 2, ntx, nsc), ("x", "core", "tx", "scan"))
    rows = ("x", "core")
    placed = (
        P(None, None, rows, "tx"),
        P(),
        P(),
        P(rows, "tx", "scan", None),
        P(rows, "tx", "scan"),
        P(rows, "tx", "scan", None, None),
    )
    return jax.shard_map(
        functools.partial(per_device, (ny // 2, ntx, nsc)),
        mesh=split,
        in_specs=placed,
        out_specs=(P(None, None, rows, "tx"), P()),
        check_vma=False,
    )
```

```python
import functools

import jax
import jax.numpy as jnp
import numpy as np
from jax import lax
from jax.experimental import pallas as pl
from jax.experimental.pallas import tpu as pltpu
from jax.sharding import Mesh
from jax.sharding import PartitionSpec as P

F32 = jnp.float32
BF16 = jnp.bfloat16
VMEM = pl.BlockSpec(memory_space=pltpu.VMEM)
SMEM = pl.BlockSpec(memory_space=pltpu.SMEM)
ANY = pl.BlockSpec(memory_space=pl.ANY)
LONG = 10**10
CODE = 512
STEPS = (0, 2, 1, 3)
PARAMS = pltpu.CompilerParams(vmem_limit_bytes=48 * 1024 * 1024)
W = 128
HALF = 64
TILE = 256
MODES = 4


def call(body, outs, args, specs, scratch=(), name=None, flops=0):
    return pl.pallas_call(
        body,
        out_shape=[jax.ShapeDtypeStruct(shape, F32) for shape in outs],
        in_specs=specs,
        out_specs=[VMEM] * len(outs),
        scratch_shapes=list(scratch),
        compiler_params=PARAMS,
        cost_estimate=pl.CostEstimate(flops=flops, bytes_accessed=0, transcendentals=0) if flops else None,
        name=name,
    )(*args)


def copy_all(pairs, sems):
    copies = [
        pltpu.make_async_copy(source, target, sems.at[k])
        for k, (source, target) in enumerate(pairs)
    ]
    for copy in copies:
        copy.start()
    for copy in copies:
        copy.wait()


def low_lanes(rows):
    return lax.broadcasted_iota(jnp.int32, (rows, W), 1) < HALF


def swap(x):
    return pltpu.roll(x, HALF, 1)


def rim_rows(core, last):
    return pl.multiple_of((1 - core) * last, HALF), pl.multiple_of(core * last, HALF)


def fold_corner(rows, left, right):
    short = low_lanes(HALF // 2)
    upper, lower = rows[: HALF // 2], rows[HALF // 2 :]
    left[...] = jnp.where(short, upper[:, :W], swap(lower[:, :W]))
    right[...] = jnp.where(short, swap(upper[:, W:]), lower[:, W:])


def right_body(tile, to_right):
    wide = low_lanes(W)
    for part in range(4):
        first, second = tile[part, :W, W:], tile[part, W:, W:]
        to_right[part] = jnp.where(wide, swap(first), second)


def left_body(tile, after, to_left):
    wide = low_lanes(W)
    for part in range(4):
        first, second = tile[part, :W, :W], tile[part, W:, :W]
        to_left[part] = jnp.where(wide, first, swap(second))


def strips_body(tile, after, to_core, to_far, far_left, far_right):
    core_row, far_row = rim_rows(lax.axis_index("core"), TILE - HALF)
    for part in range(4):
        to_core[part] = tile[part, pl.ds(core_row, HALF), :]
        rows = tile[part, pl.ds(far_row, HALF), :]
        to_far[part] = rows
        fold_corner(rows, far_left.at[part], far_right.at[part])


def corners_body(from_right, from_left, out):
    core = lax.axis_index("core")
    low = low_lanes(HALF)
    span = pl.ds(pl.multiple_of((1 - core) * HALF, HALF), HALF)
    for part in range(4):
        right, left = from_right[part, span], from_left[part, span]
        right = jnp.where(core == 0, swap(right), right)
        left = jnp.where(core == 0, left, swap(left))
        out[part] = jnp.where(low, right, left)


def guard_body(far, right, left, mark):
    mark[...] = jnp.zeros_like(mark)


def phase_body(phase, real, imag):
    real[...] = jnp.cos(phase[...])
    imag[...] = jnp.sin(phase[...])


def halves(x):
    high = x.astype(BF16)
    return high, (x - high.astype(F32)).astype(BF16)


def times_right(real, imag, table):
    outs = ([], [])
    for k in range(0, len(real), 2):
        high, low = halves(
            jnp.concatenate(
                [jnp.concatenate([r, i], axis=1) for r, i in zip(real[k : k + 2], imag[k : k + 2])],
                axis=0,
            )
        )
        out = jnp.dot(jnp.concatenate([high, low, high], axis=1), table, preferred_element_type=F32)
        for m in range(2):
            outs[0].append(out[W * m : W * (m + 1), :W])
            outs[1].append(out[W * m : W * (m + 1), W:])
    return outs


def times_left(table, real, imag):
    outs = ([], [])
    for k in range(0, len(real), 2):
        high, low = halves(
            jnp.concatenate(
                [jnp.concatenate(real[k : k + 2], axis=1), jnp.concatenate(imag[k : k + 2], axis=1)],
                axis=0,
            )
        )
        out = jnp.dot(table, jnp.concatenate([high, low, high], axis=0), preferred_element_type=F32)
        for m in range(2):
            outs[0].append(out[:W, W * m : W * (m + 1)])
            outs[1].append(out[W:, W * m : W * (m + 1)])
    return outs


def slots_body(
    starts,
    live_counts,
    tile,
    from_right,
    from_left,
    from_core,
    from_far,
    far_right,
    far_left,
    corners,
    mark,
    probe,
    kernel_real,
    kernel_imag,
    measured,
    right_high,
    right_low,
    left_high,
    left_low,
    out0,
    out1,
    out2,
    out3,
    probe_send,
    probe_keep,
    wide,
    grads,
    probe_sum,
    mid,
    patches,
):
    core, scan = lax.axis_index("core"), lax.axis_index("scan")
    live = live_counts[0, 0, 0]
    core_row, far_row = rim_rows(core, TILE + HALF)
    tall = low_lanes(W)
    short = low_lanes(HALF // 2)
    for part in range(4):
        wide[part, 0, HALF : HALF + TILE] = tile[part, :, :W]
        wide[part, 1, HALF : HALF + TILE] = tile[part, :, W:]
        right, left = from_right[part], from_left[part]
        wide[part, 2, HALF : HALF + W] = jnp.where(tall, right, swap(left))
        wide[part, 2, HALF + W : HALF + TILE] = jnp.where(tall, swap(right), left)
        for row, strip in ((core_row, from_core), (far_row, from_far)):
            wide[part, 0, pl.ds(row, HALF)] = strip[part, :, :W]
            wide[part, 1, pl.ds(row, HALF)] = strip[part, :, W:]
        wide[part, 2, pl.ds(core_row, HALF)] = corners[part]
        right, left = far_right[part], far_left[part]
        wide[part, 2, pl.ds(far_row, HALF // 2)] = jnp.where(short, right, swap(left))
        lower = pl.multiple_of(far_row + HALF // 2, HALF // 2)
        wide[part, 2, pl.ds(lower, HALF // 2)] = jnp.where(short, swap(right), left)

    def corner(slot):
        return starts[2 * slot], starts[2 * slot + 1]

    forward_right = jnp.concatenate([right_high[...], right_high[...], right_low[...]], axis=0)
    inverse_right = jnp.concatenate([left_high[...], left_high[...], left_low[...]], axis=0)
    forward_left = jnp.concatenate([left_high[...], left_high[...], left_low[...]], axis=1)
    inverse_left = jnp.concatenate([right_high[...], right_high[...], right_low[...]], axis=1)

    def transform(real, imag):
        return times_left(forward_left, *times_right(real, imag, forward_right))

    def untransform(real, imag):
        return times_right(*times_left(inverse_left, real, imag), inverse_right)

    modes = range(MODES)
    lanes = lax.broadcasted_iota(jnp.int32, (W, W), 1)

    for slot in range(2):
        row, col = corner(slot)
        block = col // W
        shift = col - block * W
        after = jnp.where(block == 2, 0, block + 1)
        turn = jnp.where(shift == 0, 0, W - shift)
        for part in range(4):
            one = pltpu.roll(wide[part, block, pl.ds(row, W)], turn, 1)
            two = pltpu.roll(wide[part, after, pl.ds(row, W)], turn, 1)
            patches[4 * slot + part] = jnp.where(lanes < W - shift, one, two)
    slots = range(2)
    pairs = [(slot, m) for slot in slots for m in modes]

    def patch(part):
        return [patches[4 * slot + part] for slot in slots]

    def times(real, imag, by_real, by_imag):
        return (
            [r * by_real[s] - i * by_imag[s] for (s, m), r, i in zip(pairs, real, imag)],
            [r * by_imag[s] + i * by_real[s] for (s, m), r, i in zip(pairs, real, imag)],
        )

    def times_conj(real, imag, by_real, by_imag):
        return (
            [r * by_real[s] + i * by_imag[s] for (s, m), r, i in zip(pairs, real, imag)],
            [i * by_real[s] - r * by_imag[s] for (s, m), r, i in zip(pairs, real, imag)],
        )

    def total(terms):
        return [functools.reduce(jnp.add, terms[MODES * s : MODES * (s + 1)]) for s in slots]

    near_real, near_imag = patch(0), patch(1)
    real, imag = times(
        [probe[2 * m] for s, m in pairs], [probe[2 * m + 1] for s, m in pairs], near_real, near_imag
    )
    real, imag = transform(real, imag)
    kr, ki = [kernel_real[...]] * 2, [kernel_imag[...]] * 2
    real, imag = times(real, imag, kr, ki)
    real, imag = untransform(real, imag)
    for n in range(2 * MODES):
        mid[2 * n] = real[n]
        mid[2 * n + 1] = imag[n]
    away_real, away_imag = patch(2), patch(3)
    real, imag = times(real, imag, away_real, away_imag)
    real, imag = transform(real, imag)
    intensity = total([r * r + i * i for r, i in zip(real, imag)])
    residual = [
        (intensity[s] - measured[s]) * jnp.where(s < live, 2.0, 0.0).astype(F32) for s in slots
    ]
    real = [r * residual[s] for (s, m), r in zip(pairs, real)]
    imag = [i * residual[s] for (s, m), i in zip(pairs, imag)]
    real, imag = untransform(real, imag)
    both = range(2 * MODES)
    grad_real = total([mid[2 * n] * real[n] + mid[2 * n + 1] * imag[n] for n in both])
    grad_imag = total([mid[2 * n] * imag[n] - mid[2 * n + 1] * real[n] for n in both])
    for s in slots:
        grads[2, s] = grad_real[s]
        grads[3, s] = grad_imag[s]
    real, imag = times_conj(real, imag, patch(2), patch(3))
    real, imag = transform(real, imag)
    real, imag = times_conj(real, imag, kr, ki)
    real, imag = untransform(real, imag)
    grad_real = total([probe[2 * m] * real[n] + probe[2 * m + 1] * imag[n] for n, (s, m) in enumerate(pairs)])
    grad_imag = total([probe[2 * m] * imag[n] - probe[2 * m + 1] * real[n] for n, (s, m) in enumerate(pairs)])
    for s in slots:
        grads[0, s] = grad_real[s]
        grads[1, s] = grad_imag[s]
    real, imag = times_conj(real, imag, patch(0), patch(1))
    for m in modes:
        probe_sum[2 * m] = real[m] + real[MODES + m]
        probe_sum[2 * m + 1] = imag[m] + imag[MODES + m]

    places = lax.broadcasted_iota(jnp.int32, (8, W), 0)
    marks = jnp.zeros((8, W), F32)
    for slot in range(2):
        row, col = corner(slot)
        marks = jnp.where(places == slot, (row * CODE + col).astype(F32), marks)
    for step, out in enumerate((out0, out1, out2, out3)):
        part = lax.rem(scan + step, 4)
        for slot in range(2):
            out[W * slot : W * (slot + 1)] = grads[part, slot]
        out[2 * W :] = marks
    count = jnp.zeros((8, W), F32) + live.astype(F32)
    for half, out in ((core, probe_keep), (1 - core, probe_send)):
        for k in range(MODES):
            out[W * k : W * (k + 1)] = probe_sum[half * MODES + k]
        out[MODES * W :] = count


def spread_body(keep, got, out):
    rows = out.shape[1] - 8
    count = keep[MODES * W :] + got[MODES * W :]
    for k in range(out.shape[0]):
        span = slice(k * rows, (k + 1) * rows)
        out[k, :rows] = keep[span] + got[span]
        out[k, rows:] = count


def sum_body(chunks, after, out):
    out[...] = functools.reduce(jnp.add, [chunks[k] for k in range(chunks.shape[0])])


def pair_body(own, got, after, out):
    out[...] = own[...] + got[...]


def mean_body(own, got, spread):
    total = own[...] + got[...]
    rows = spread.shape[1]
    mean = total[:rows] / total[rows : rows + 1]
    for k in range(spread.shape[0]):
        spread[k] = mean


def place_body(one, two, three, four, to_left, to_right, wide):
    messages = (one, two, three, four)
    spots = []
    for message in messages:
        for slot in range(2):
            code = jnp.max(message[2 * W + slot : 2 * W + slot + 1]).astype(jnp.int32)
            row, col = code // CODE, lax.rem(code, CODE)
            row = jnp.clip(row, 0, TILE)
            col = jnp.clip(col, 0, 3 * W - 1)
            block = col // W
            after = jnp.where(block == 2, 0, block + 1)
            spots.append((row, block, after, col - block * W))
    wide[...] = jnp.zeros_like(wide)
    lanes = lax.broadcasted_iota(jnp.int32, (W, W), 1)
    for k, message in enumerate(messages):
        for slot in range(2):
            row, block, after, shift = spots[2 * k + slot]
            turned = pltpu.roll(message[W * slot : W * (slot + 1)], shift, 1)
            wide[block, pl.ds(row, W)] += jnp.where(lanes >= shift, turned, 0.0)
            wide[after, pl.ds(row, W)] += jnp.where(lanes < shift, turned, 0.0)
    half = (TILE + 2 * HALF) // 2
    low = low_lanes(half)
    upper, lower = wide[2, :half], wide[2, half:]
    to_right[...] = jnp.where(low, upper, swap(lower))
    to_left[...] = jnp.where(low, swap(upper), lower)


def rows_body(from_left, from_right, held, after, to_core, to_far, keep, wide):
    half = (TILE + 2 * HALF) // 2
    low = low_lanes(half)
    left, right = from_left[...], from_right[...]
    wide[0, :half] = held[0, :half] + jnp.where(low, left, 0.0)
    wide[0, half:] = held[0, half:] + jnp.where(low, swap(left), 0.0)
    wide[1, :half] = held[1, :half] + jnp.where(low, 0.0, swap(right))
    wide[1, half:] = held[1, half:] + jnp.where(low, 0.0, right)
    core_row, far_row = rim_rows(lax.axis_index("core"), TILE + HALF)
    for k in range(2):
        to_core[k] = wide[k, pl.ds(core_row, HALF)]
        to_far[k] = wide[k, pl.ds(far_row, HALF)]
        keep[k] = wide[k, HALF : HALF + TILE]


def finish_body(from_core, from_far, held, after, out):
    core_row, far_row = rim_rows(lax.axis_index("core"), TILE - HALF)
    for k in range(2):
        span = slice(k * W, (k + 1) * W)
        out[:, span] = held[k]
        out[pl.ds(core_row, HALF), span] += from_core[k]
        out[pl.ds(far_row, HALF), span] += from_far[k]


def gather_body(one, two, three, four, mine, object_grad, probe_grad, sems):
    scan, core = lax.axis_index("scan"), lax.axis_index("core")
    parts = zip(STEPS, (one, two, three, four))
    pairs = [(part, object_grad.at[lax.rem(scan + 4 - step, 4)]) for step, part in parts]
    copy_all(pairs + [(mine, probe_grad.at[core])], sems)


def other_body(probe_grad, other, out, sems):
    copy_all([(other, out.at[1 - lax.axis_index("core")])], sems)


def place_parts(body, shapes, parts, name, aliases=None):
    return pl.pallas_call(
        body,
        out_shape=[jax.ShapeDtypeStruct(shape, F32) for shape in shapes],
        in_specs=[ANY] * len(parts),
        out_specs=[ANY] * len(shapes),
        scratch_shapes=[pltpu.SemaphoreType.DMA((len(parts),))],
        compiler_params=PARAMS,
        cost_estimate=pl.CostEstimate(flops=LONG, bytes_accessed=0, transcendentals=0),
        input_output_aliases=aliases or {},
        name=name,
    )(*parts)


def tables():
    index = np.arange(W)
    angle = 2.0 * np.pi * ((index[:, None] * index[None, :]) % W) / W
    cos, sin = np.cos(angle) / np.sqrt(W), -np.sin(angle) / np.sqrt(W)
    right = np.block([[cos, sin], [-sin, cos]])
    arrays = []
    for table in (right, right.T):
        high = table.astype(BF16)
        low = (table - high.astype(np.float64)).astype(BF16)
        arrays += [high, low]
    return [jnp.asarray(a) for a in arrays]


def run_slots(*args):
    message = (2 * W + 8, W)
    share = (MODES * W + 8, W)
    return call(
        slots_body,
        [message] * 4 + [share] * 2,
        (*args, *tables()),
        [SMEM] * 2 + [VMEM] * 8 + [ANY] + [VMEM] * 8,
        scratch=[
            pltpu.VMEM((4, 3, TILE + 2 * HALF, W), F32),
            pltpu.VMEM((4, 2, W, W), F32),
            pltpu.VMEM((2 * MODES, W, W), F32),
            pltpu.VMEM((4 * MODES, W, W), F32),
            pltpu.VMEM((8, W, W), F32),
        ],
        name="slots",
    )


def per_device(sizes, specimen, probe_modes, kernel_phase, offsets, live_counts, measured):
    nx, ntx, nsc = sizes

    def over_grid(target):
        pairs = []
        for x in range(nx):
            for c in range(2):
                for t in range(ntx):
                    x2, c2, t2 = target(x, c, t)
                    pairs.append(((x * 2 + c) * ntx + t, ((x2 % nx) * 2 + c2) * ntx + t2 % ntx))
        return lambda value: lax.ppermute(value, ("x", "core", "tx"), pairs)

    def across(x, c):
        return x + (1 if c else -1), 1 - c

    to_left = over_grid(lambda x, c, t: (x, c, t - 1))
    to_right = over_grid(lambda x, c, t: (x, c, t + 1))
    to_core = over_grid(lambda x, c, t: (x, 1 - c, t))
    to_far = over_grid(lambda x, c, t: (*across(x, c), t))
    far_left = over_grid(lambda x, c, t: (*across(x, c), t - 1))
    far_right = over_grid(lambda x, c, t: (*across(x, c), t + 1))

    def to_scan(value, step):
        return lax.ppermute(value, "scan", [(s, (s + step) % nsc) for s in range(nsc)])

    def to_pair(value, mask):
        return lax.ppermute(value, "tx", [(t, t ^ mask) for t in range(ntx)])

    tile = specimen.reshape(4, TILE, TILE)
    strip, corner, side = (4, HALF, TILE), (4, HALF // 2, W), (4, W, W)
    (right,) = call(right_body, [side], (tile,), [VMEM], name="right")
    (left,) = call(left_body, [side], (tile, right), [VMEM, ANY], name="left", flops=LONG)
    near, far, corner_left, corner_right = call(
        strips_body,
        [strip, strip, corner, corner],
        (tile, left),
        [VMEM, ANY],
        name="strips",
        flops=LONG,
    )
    from_right, from_left = to_left(left), to_right(right)
    from_core, from_far = to_core(near), to_far(far)
    corner_right, corner_left = far_left(corner_left), far_right(corner_right)
    (corners,) = call(
        corners_body, [(4, HALF, W)], (from_right, from_left), [VMEM] * 2, name="corners"
    )
    corners = to_core(corners)
    (mark,) = call(
        guard_body,
        [(8, W)],
        (from_far, corner_right, corner_left),
        [ANY] * 3,
        name="guard",
        flops=LONG,
    )
    kernel_real, kernel_imag = call(
        phase_body, [(W, W)] * 2, (kernel_phase,), [VMEM], name="phase"
    )
    rows = jnp.clip(offsets[0, 0, :, 0] + HALF, 0, TILE)
    cols = jnp.clip(offsets[0, 0, :, 1], -HALF, TILE - HALF)
    starts = jnp.stack([rows, jnp.where(cols < 0, cols + 3 * W, cols)], axis=1).reshape(4)
    outs = run_slots(
        starts,
        live_counts,
        tile,
        from_right,
        from_left,
        from_core,
        from_far,
        corner_right,
        corner_left,
        corners,
        mark,
        probe_modes.reshape(2 * MODES, W, W),
        kernel_real,
        kernel_imag,
        measured[0, 0],
    )
    own, away, probe_send, probe_keep = outs[0], outs[1:4], outs[4], outs[5]
    arrived = [to_scan(value, step) for step, value in enumerate(away, 1)]
    probe_got = to_core(probe_send)
    peers = nx * nsc
    rows = MODES * W // peers
    (chunks,) = call(
        spread_body,
        [(peers, rows + 8, W)],
        (probe_keep, probe_got),
        [VMEM] * 2,
        name="spread",
        flops=LONG,
    )
    chunks = lax.all_to_all(chunks, ("x", "scan"), 0, 0)
    tall = TILE + 2 * HALF
    left, right, held = call(
        place_body,
        [(tall // 2, W)] * 2 + [(3, tall, W)],
        (own, *arrived),
        [VMEM] * 4,
        name="place",
        flops=LONG,
    )
    (share,) = call(
        sum_body, [(rows + 8, W)], (chunks, left), [VMEM, ANY], name="sum", flops=LONG
    )
    left, right = to_left(left), to_right(right)
    got = to_pair(share, 1)
    near, far, held = call(
        rows_body,
        [(2, HALF, W)] * 2 + [(2, TILE, W)],
        (right, left, held, share),
        [VMEM] * 3 + [ANY],
        scratch=[pltpu.VMEM((2, tall, W), F32)],
        name="rows",
        flops=LONG,
    )
    (share,) = call(
        pair_body, [(rows + 8, W)], (share, got, near), [VMEM] * 2 + [ANY], name="pair", flops=LONG
    )
    got = to_pair(share, 2)
    near, far = to_core(near), to_far(far)
    (quarter,) = call(
        finish_body,
        [(TILE, TILE)],
        (near, far, held, share),
        [VMEM] * 3 + [ANY],
        name="finish",
        flops=LONG,
    )
    quarters = [quarter] + [to_scan(quarter, step) for step in STEPS[1:]]
    (share,) = call(
        pair_body, [(rows + 8, W)], (share, got, quarter), [VMEM] * 2 + [ANY], name="pair", flops=LONG
    )
    got = to_pair(share, ntx - 1)
    (spread,) = call(
        mean_body,
        [(peers, rows, W)],
        (share, got),
        [VMEM] * 2,
        name="mean",
        flops=LONG,
    )
    mine = lax.all_to_all(spread, ("x", "scan"), 0, 0).reshape(MODES * W, W)
    other = to_core(mine)
    both = (2, MODES * W, W)
    object_grad, probe_grad = place_parts(
        gather_body, [(4, TILE, TILE), both], (*quarters, mine), "gather"
    )
    (probe_grad,) = place_parts(other_body, [both], (probe_grad, other), "other", {0: 0})
    return object_grad.reshape(specimen.shape), probe_grad.reshape(probe_modes.shape)


def solution(mesh):
    ny, ntx, nsc = mesh.devices.shape
    split = Mesh(mesh.devices.reshape(ny // 2, 2, ntx, nsc), ("x", "core", "tx", "scan"))
    rows = ("x", "core")
    placed = (
        P(None, None, rows, "tx"),
        P(),
        P(),
        P(rows, "tx", "scan", None),
        P(rows, "tx", "scan"),
        P(rows, "tx", "scan", None, None),
    )
    return jax.shard_map(
        functools.partial(per_device, (ny // 2, ntx, nsc)),
        mesh=split,
        in_specs=placed,
        out_specs=(P(None, None, rows, "tx"), P()),
        check_vma=False,
    )
```

```python
import functools

import jax
import jax.numpy as jnp
import numpy as np
from jax import lax
from jax.experimental import pallas as pl
from jax.experimental.pallas import tpu as pltpu
from jax.sharding import Mesh
from jax.sharding import PartitionSpec as P

F32 = jnp.float32
BF16 = jnp.bfloat16
VMEM = pl.BlockSpec(memory_space=pltpu.VMEM)
SMEM = pl.BlockSpec(memory_space=pltpu.SMEM)
ANY = pl.BlockSpec(memory_space=pl.ANY)
LONG = 10**10
CODE = 512
STEPS = (0, 2, 1, 3)
PARAMS = pltpu.CompilerParams(vmem_limit_bytes=48 * 1024 * 1024)
W = 128
HALF = 64
TILE = 256
MODES = 4


def call(body, outs, args, specs, scratch=(), name=None, flops=0):
    return pl.pallas_call(
        body,
        out_shape=[jax.ShapeDtypeStruct(shape, F32) for shape in outs],
        in_specs=specs,
        out_specs=[VMEM] * len(outs),
        scratch_shapes=list(scratch),
        compiler_params=PARAMS,
        cost_estimate=pl.CostEstimate(flops=flops, bytes_accessed=0, transcendentals=0) if flops else None,
        name=name,
    )(*args)


def copy_all(pairs, sems):
    copies = [
        pltpu.make_async_copy(source, target, sems.at[k])
        for k, (source, target) in enumerate(pairs)
    ]
    for copy in copies:
        copy.start()
    for copy in copies:
        copy.wait()


def low_lanes(rows):
    return lax.broadcasted_iota(jnp.int32, (rows, W), 1) < HALF


def swap(x):
    return pltpu.roll(x, HALF, 1)


def rim_rows(core, last):
    return pl.multiple_of((1 - core) * last, HALF), pl.multiple_of(core * last, HALF)


def fold_corner(rows, left, right):
    short = low_lanes(HALF // 2)
    upper, lower = rows[: HALF // 2], rows[HALF // 2 :]
    left[...] = jnp.where(short, upper[:, :W], swap(lower[:, :W]))
    right[...] = jnp.where(short, swap(upper[:, W:]), lower[:, W:])


def right_body(tile, to_right):
    wide = low_lanes(W)
    for part in range(4):
        first, second = tile[part, :W, W:], tile[part, W:, W:]
        to_right[part] = jnp.where(wide, swap(first), second)


def left_body(tile, after, to_left):
    wide = low_lanes(W)
    for part in range(4):
        first, second = tile[part, :W, :W], tile[part, W:, :W]
        to_left[part] = jnp.where(wide, first, swap(second))


def strips_body(tile, after, to_core, to_far, far_left, far_right):
    core_row, far_row = rim_rows(lax.axis_index("core"), TILE - HALF)
    for part in range(4):
        to_core[part] = tile[part, pl.ds(core_row, HALF), :]
        rows = tile[part, pl.ds(far_row, HALF), :]
        to_far[part] = rows
        fold_corner(rows, far_left.at[part], far_right.at[part])


def corners_body(from_right, from_left, out):
    core = lax.axis_index("core")
    low = low_lanes(HALF)
    span = pl.ds(pl.multiple_of((1 - core) * HALF, HALF), HALF)
    for part in range(4):
        right, left = from_right[part, span], from_left[part, span]
        right = jnp.where(core == 0, swap(right), right)
        left = jnp.where(core == 0, left, swap(left))
        out[part] = jnp.where(low, right, left)


def guard_body(far, right, left, mark):
    mark[...] = jnp.zeros_like(mark)


def phase_body(phase, real, imag):
    real[...] = jnp.cos(phase[...])
    imag[...] = jnp.sin(phase[...])


def halves(x):
    high = x.astype(BF16)
    return high, (x - high.astype(F32)).astype(BF16)


def times_right(real, imag, table):
    outs = ([], [])
    for k in range(0, len(real), 2):
        high, low = halves(
            jnp.concatenate(
                [jnp.concatenate([r, i], axis=1) for r, i in zip(real[k : k + 2], imag[k : k + 2])],
                axis=0,
            )
        )
        out = jnp.dot(jnp.concatenate([high, low, high], axis=1), table, preferred_element_type=F32)
        for m in range(2):
            outs[0].append(out[W * m : W * (m + 1), :W])
            outs[1].append(out[W * m : W * (m + 1), W:])
    return outs


def times_left(table, real, imag):
    outs = ([], [])
    for k in range(0, len(real), 2):
        high, low = halves(
            jnp.concatenate(
                [jnp.concatenate(real[k : k + 2], axis=1), jnp.concatenate(imag[k : k + 2], axis=1)],
                axis=0,
            )
        )
        out = jnp.dot(table, jnp.concatenate([high, low, high], axis=0), preferred_element_type=F32)
        for m in range(2):
            outs[0].append(out[:W, W * m : W * (m + 1)])
            outs[1].append(out[W:, W * m : W * (m + 1)])
    return outs


def slots_body(
    starts,
    live_counts,
    tile,
    from_right,
    from_left,
    from_core,
    from_far,
    far_right,
    far_left,
    corners,
    mark,
    probe,
    kernel_real,
    kernel_imag,
    measured,
    right_high,
    right_low,
    left_high,
    left_low,
    out0,
    out1,
    out2,
    out3,
    probe_send,
    probe_keep,
    wide,
    grads,
    probe_sum,
    mid,
    patches,
):
    core, scan = lax.axis_index("core"), lax.axis_index("scan")
    live = live_counts[0, 0, 0]
    core_row, far_row = rim_rows(core, TILE + HALF)
    tall = low_lanes(W)
    short = low_lanes(HALF // 2)
    for part in range(4):
        wide[part, 0, HALF : HALF + TILE] = tile[part, :, :W]
        wide[part, 1, HALF : HALF + TILE] = tile[part, :, W:]
        right, left = from_right[part], from_left[part]
        wide[part, 2, HALF : HALF + W] = jnp.where(tall, right, swap(left))
        wide[part, 2, HALF + W : HALF + TILE] = jnp.where(tall, swap(right), left)
        for row, strip in ((core_row, from_core), (far_row, from_far)):
            wide[part, 0, pl.ds(row, HALF)] = strip[part, :, :W]
            wide[part, 1, pl.ds(row, HALF)] = strip[part, :, W:]
        wide[part, 2, pl.ds(core_row, HALF)] = corners[part]
        right, left = far_right[part], far_left[part]
        wide[part, 2, pl.ds(far_row, HALF // 2)] = jnp.where(short, right, swap(left))
        lower = pl.multiple_of(far_row + HALF // 2, HALF // 2)
        wide[part, 2, pl.ds(lower, HALF // 2)] = jnp.where(short, swap(right), left)

    def corner(slot):
        return starts[2 * slot], starts[2 * slot + 1]

    forward_right = jnp.concatenate([right_high[...], right_high[...], right_low[...]], axis=0)
    inverse_right = jnp.concatenate([left_high[...], left_high[...], left_low[...]], axis=0)
    forward_left = jnp.concatenate([left_high[...], left_high[...], left_low[...]], axis=1)
    inverse_left = jnp.concatenate([right_high[...], right_high[...], right_low[...]], axis=1)

    def transform(real, imag):
        return times_left(forward_left, *times_right(real, imag, forward_right))

    def untransform(real, imag):
        return times_right(*times_left(inverse_left, real, imag), inverse_right)

    modes = range(MODES)
    lanes = lax.broadcasted_iota(jnp.int32, (W, W), 1)

    for slot in range(2):
        row, col = corner(slot)
        block = col // W
        shift = col - block * W
        after = jnp.where(block == 2, 0, block + 1)
        turn = jnp.where(shift == 0, 0, W - shift)
        for part in range(4):
            one = pltpu.roll(wide[part, block, pl.ds(row, W)], turn, 1)
            two = pltpu.roll(wide[part, after, pl.ds(row, W)], turn, 1)
            patches[4 * slot + part] = jnp.where(lanes < W - shift, one, two)
    slots = range(2)
    pairs = [(slot, m) for slot in slots for m in modes]

    def patch(part):
        return [patches[4 * slot + part] for slot in slots]

    def times(real, imag, by_real, by_imag):
        return (
            [r * by_real[s] - i * by_imag[s] for (s, m), r, i in zip(pairs, real, imag)],
            [r * by_imag[s] + i * by_real[s] for (s, m), r, i in zip(pairs, real, imag)],
        )

    def times_conj(real, imag, by_real, by_imag):
        return (
            [r * by_real[s] + i * by_imag[s] for (s, m), r, i in zip(pairs, real, imag)],
            [i * by_real[s] - r * by_imag[s] for (s, m), r, i in zip(pairs, real, imag)],
        )

    def total(terms):
        return [functools.reduce(jnp.add, terms[MODES * s : MODES * (s + 1)]) for s in slots]

    near_real, near_imag = patch(0), patch(1)
    real, imag = times(
        [probe[2 * m] for s, m in pairs], [probe[2 * m + 1] for s, m in pairs], near_real, near_imag
    )
    real, imag = transform(real, imag)
    kr, ki = [kernel_real[...]] * 2, [kernel_imag[...]] * 2
    real, imag = times(real, imag, kr, ki)
    real, imag = untransform(real, imag)
    for n in range(2 * MODES):
        mid[2 * n] = real[n]
        mid[2 * n + 1] = imag[n]
    away_real, away_imag = patch(2), patch(3)
    real, imag = times(real, imag, away_real, away_imag)
    real, imag = transform(real, imag)
    intensity = total([r * r + i * i for r, i in zip(real, imag)])
    residual = [
        (intensity[s] - measured[s]) * jnp.where(s < live, 2.0, 0.0).astype(F32) for s in slots
    ]
    real = [r * residual[s] for (s, m), r in zip(pairs, real)]
    imag = [i * residual[s] for (s, m), i in zip(pairs, imag)]
    real, imag = untransform(real, imag)
    both = range(2 * MODES)
    grad_real = total([mid[2 * n] * real[n] + mid[2 * n + 1] * imag[n] for n in both])
    grad_imag = total([mid[2 * n] * imag[n] - mid[2 * n + 1] * real[n] for n in both])
    for s in slots:
        grads[2, s] = grad_real[s]
        grads[3, s] = grad_imag[s]
    real, imag = times_conj(real, imag, patch(2), patch(3))
    real, imag = transform(real, imag)
    real, imag = times_conj(real, imag, kr, ki)
    real, imag = untransform(real, imag)
    grad_real = total([probe[2 * m] * real[n] + probe[2 * m + 1] * imag[n] for n, (s, m) in enumerate(pairs)])
    grad_imag = total([probe[2 * m] * imag[n] - probe[2 * m + 1] * real[n] for n, (s, m) in enumerate(pairs)])
    for s in slots:
        grads[0, s] = grad_real[s]
        grads[1, s] = grad_imag[s]
    real, imag = times_conj(real, imag, patch(0), patch(1))
    for m in modes:
        probe_sum[2 * m] = real[m] + real[MODES + m]
        probe_sum[2 * m + 1] = imag[m] + imag[MODES + m]

    places = lax.broadcasted_iota(jnp.int32, (8, W), 0)
    marks = jnp.zeros((8, W), F32)
    for slot in range(2):
        row, col = corner(slot)
        marks = jnp.where(places == slot, (row * CODE + col).astype(F32), marks)
    for step, out in enumerate((out0, out1, out2, out3)):
        part = lax.rem(scan + step, 4)
        for slot in range(2):
            out[W * slot : W * (slot + 1)] = grads[part, slot]
        out[2 * W :] = marks
    count = jnp.zeros((8, W), F32) + live.astype(F32)
    for half, out in ((core, probe_keep), (1 - core, probe_send)):
        for k in range(MODES):
            out[W * k : W * (k + 1)] = probe_sum[half * MODES + k]
        out[MODES * W :] = count


def spread_body(keep, got, out):
    rows = out.shape[1] - 8
    count = keep[MODES * W :] + got[MODES * W :]
    for k in range(out.shape[0]):
        span = slice(k * rows, (k + 1) * rows)
        out[k, :rows] = keep[span] + got[span]
        out[k, rows:] = count


def sum_body(chunks, after, out):
    out[...] = functools.reduce(jnp.add, [chunks[k] for k in range(chunks.shape[0])])


def pair_body(own, got, after, out):
    out[...] = own[...] + got[...]


def mean_body(own, got, spread):
    total = own[...] + got[...]
    rows = spread.shape[1]
    mean = total[:rows] / total[rows : rows + 1]
    for k in range(spread.shape[0]):
        spread[k] = mean


def place_body(one, two, three, four, to_left, to_right, wide):
    messages = (one, two, three, four)
    spots = []
    for message in messages:
        for slot in range(2):
            code = jnp.max(message[2 * W + slot : 2 * W + slot + 1]).astype(jnp.int32)
            row, col = code // CODE, lax.rem(code, CODE)
            row = jnp.clip(row, 0, TILE)
            col = jnp.clip(col, 0, 3 * W - 1)
            block = col // W
            after = jnp.where(block == 2, 0, block + 1)
            spots.append((row, block, after, col - block * W))
    wide[...] = jnp.zeros_like(wide)
    lanes = lax.broadcasted_iota(jnp.int32, (W, W), 1)
    for k, message in enumerate(messages):
        for slot in range(2):
            row, block, after, shift = spots[2 * k + slot]
            turned = pltpu.roll(message[W * slot : W * (slot + 1)], shift, 1)
            wide[block, pl.ds(row, W)] += jnp.where(lanes >= shift, turned, 0.0)
            wide[after, pl.ds(row, W)] += jnp.where(lanes < shift, turned, 0.0)
    half = (TILE + 2 * HALF) // 2
    low = low_lanes(half)
    upper, lower = wide[2, :half], wide[2, half:]
    to_right[...] = jnp.where(low, upper, swap(lower))
    to_left[...] = jnp.where(low, swap(upper), lower)


def rows_body(from_left, from_right, held, after, to_core, to_far, keep, wide):
    half = (TILE + 2 * HALF) // 2
    low = low_lanes(half)
    left, right = from_left[...], from_right[...]
    wide[0, :half] = held[0, :half] + jnp.where(low, left, 0.0)
    wide[0, half:] = held[0, half:] + jnp.where(low, swap(left), 0.0)
    wide[1, :half] = held[1, :half] + jnp.where(low, 0.0, swap(right))
    wide[1, half:] = held[1, half:] + jnp.where(low, 0.0, right)
    core_row, far_row = rim_rows(lax.axis_index("core"), TILE + HALF)
    for k in range(2):
        to_core[k] = wide[k, pl.ds(core_row, HALF)]
        to_far[k] = wide[k, pl.ds(far_row, HALF)]
        keep[k] = wide[k, HALF : HALF + TILE]


def finish_body(from_core, from_far, held, after, out):
    core_row, far_row = rim_rows(lax.axis_index("core"), TILE - HALF)
    for k in range(2):
        span = slice(k * W, (k + 1) * W)
        out[:, span] = held[k]
        out[pl.ds(core_row, HALF), span] += from_core[k]
        out[pl.ds(far_row, HALF), span] += from_far[k]


def gather_body(one, two, three, four, mine, object_grad, probe_grad, sems):
    scan, core = lax.axis_index("scan"), lax.axis_index("core")
    parts = zip(STEPS, (one, two, three, four))
    pairs = [(part, object_grad.at[lax.rem(scan + 4 - step, 4)]) for step, part in parts]
    copy_all(pairs + [(mine, probe_grad.at[core])], sems)


def other_body(probe_grad, other, out, sems):
    copy_all([(other, out.at[1 - lax.axis_index("core")])], sems)


def place_parts(body, shapes, parts, name, aliases=None):
    return pl.pallas_call(
        body,
        out_shape=[jax.ShapeDtypeStruct(shape, F32) for shape in shapes],
        in_specs=[ANY] * len(parts),
        out_specs=[ANY] * len(shapes),
        scratch_shapes=[pltpu.SemaphoreType.DMA((len(parts),))],
        compiler_params=PARAMS,
        cost_estimate=pl.CostEstimate(flops=LONG, bytes_accessed=0, transcendentals=0),
        input_output_aliases=aliases or {},
        name=name,
    )(*parts)


def tables():
    index = np.arange(W)
    angle = 2.0 * np.pi * ((index[:, None] * index[None, :]) % W) / W
    cos, sin = np.cos(angle) / np.sqrt(W), -np.sin(angle) / np.sqrt(W)
    right = np.block([[cos, sin], [-sin, cos]])
    arrays = []
    for table in (right, right.T):
        high = table.astype(BF16)
        low = (table - high.astype(np.float64)).astype(BF16)
        arrays += [high, low]
    return [jnp.asarray(a) for a in arrays]


def run_slots(*args):
    message = (2 * W + 8, W)
    share = (MODES * W + 8, W)
    return call(
        slots_body,
        [message] * 4 + [share] * 2,
        (*args, *tables()),
        [SMEM] * 2 + [VMEM] * 8 + [ANY] + [VMEM] * 8,
        scratch=[
            pltpu.VMEM((4, 3, TILE + 2 * HALF, W), F32),
            pltpu.VMEM((4, 2, W, W), F32),
            pltpu.VMEM((2 * MODES, W, W), F32),
            pltpu.VMEM((4 * MODES, W, W), F32),
            pltpu.VMEM((8, W, W), F32),
        ],
        name="slots",
    )


def per_device(sizes, specimen, probe_modes, kernel_phase, offsets, live_counts, measured):
    nx, ntx, nsc = sizes

    def over_grid(target):
        pairs = []
        for x in range(nx):
            for c in range(2):
                for t in range(ntx):
                    x2, c2, t2 = target(x, c, t)
                    pairs.append(((x * 2 + c) * ntx + t, ((x2 % nx) * 2 + c2) * ntx + t2 % ntx))
        return lambda value: lax.ppermute(value, ("x", "core", "tx"), pairs)

    def across(x, c):
        return x + (1 if c else -1), 1 - c

    to_left = over_grid(lambda x, c, t: (x, c, t - 1))
    to_right = over_grid(lambda x, c, t: (x, c, t + 1))
    to_core = over_grid(lambda x, c, t: (x, 1 - c, t))
    to_far = over_grid(lambda x, c, t: (*across(x, c), t))
    far_left = over_grid(lambda x, c, t: (*across(x, c), t - 1))
    far_right = over_grid(lambda x, c, t: (*across(x, c), t + 1))

    def to_scan(value, step):
        return lax.ppermute(value, "scan", [(s, (s + step) % nsc) for s in range(nsc)])

    def to_pair(value, mask):
        return lax.ppermute(value, "tx", [(t, t ^ mask) for t in range(ntx)])

    tile = specimen.reshape(4, TILE, TILE)
    strip, corner, side = (4, HALF, TILE), (4, HALF // 2, W), (4, W, W)
    (right,) = call(right_body, [side], (tile,), [VMEM], name="right")
    (left,) = call(left_body, [side], (tile, right), [VMEM, ANY], name="left", flops=LONG)
    near, far, corner_left, corner_right = call(
        strips_body,
        [strip, strip, corner, corner],
        (tile, left),
        [VMEM, ANY],
        name="strips",
        flops=LONG,
    )
    from_right, from_left = to_left(left), to_right(right)
    from_core, from_far = to_core(near), to_far(far)
    corner_right, corner_left = far_left(corner_left), far_right(corner_right)
    (corners,) = call(
        corners_body, [(4, HALF, W)], (from_right, from_left), [VMEM] * 2, name="corners"
    )
    corners = to_core(corners)
    (mark,) = call(
        guard_body,
        [(8, W)],
        (from_far, corner_right, corner_left),
        [ANY] * 3,
        name="guard",
        flops=LONG,
    )
    kernel_real, kernel_imag = call(
        phase_body, [(W, W)] * 2, (kernel_phase,), [VMEM], name="phase"
    )
    rows = jnp.clip(offsets[0, 0, :, 0] + HALF, 0, TILE)
    cols = jnp.clip(offsets[0, 0, :, 1], -HALF, TILE - HALF)
    starts = jnp.stack([rows, jnp.where(cols < 0, cols + 3 * W, cols)], axis=1).reshape(4)
    outs = run_slots(
        starts,
        live_counts,
        tile,
        from_right,
        from_left,
        from_core,
        from_far,
        corner_right,
        corner_left,
        corners,
        mark,
        probe_modes.reshape(2 * MODES, W, W),
        kernel_real,
        kernel_imag,
        measured[0, 0],
    )
    own, away, probe_send, probe_keep = outs[0], outs[1:4], outs[4], outs[5]
    arrived = [to_scan(value, step) for step, value in enumerate(away, 1)]
    probe_got = to_core(probe_send)
    peers = nx * nsc
    rows = MODES * W // peers
    (chunks,) = call(
        spread_body,
        [(peers, rows + 8, W)],
        (probe_keep, probe_got),
        [VMEM] * 2,
        name="spread",
        flops=LONG,
    )
    chunks = lax.all_to_all(chunks, ("x", "scan"), 0, 0)
    tall = TILE + 2 * HALF
    left, right, held = call(
        place_body,
        [(tall // 2, W)] * 2 + [(3, tall, W)],
        (own, *arrived),
        [VMEM] * 4,
        name="place",
        flops=LONG,
    )
    (share,) = call(
        sum_body, [(rows + 8, W)], (chunks, left), [VMEM, ANY], name="sum", flops=LONG
    )
    left, right = to_left(left), to_right(right)
    got = to_pair(share, 2)
    near, far, held = call(
        rows_body,
        [(2, HALF, W)] * 2 + [(2, TILE, W)],
        (right, left, held, share),
        [VMEM] * 3 + [ANY],
        scratch=[pltpu.VMEM((2, tall, W), F32)],
        name="rows",
        flops=LONG,
    )
    (share,) = call(
        pair_body, [(rows + 8, W)], (share, got, near), [VMEM] * 2 + [ANY], name="pair", flops=LONG
    )
    got = to_pair(share, 1)
    near, far = to_core(near), to_far(far)
    (quarter,) = call(
        finish_body,
        [(TILE, TILE)],
        (near, far, held, share),
        [VMEM] * 3 + [ANY],
        name="finish",
        flops=LONG,
    )
    quarters = [quarter] + [to_scan(quarter, step) for step in STEPS[1:]]
    (share,) = call(
        pair_body, [(rows + 8, W)], (share, got, quarter), [VMEM] * 2 + [ANY], name="pair", flops=LONG
    )
    got = to_pair(share, ntx - 1)
    (spread,) = call(
        mean_body,
        [(peers, rows, W)],
        (share, got),
        [VMEM] * 2,
        name="mean",
        flops=LONG,
    )
    mine = lax.all_to_all(spread, ("x", "scan"), 0, 0).reshape(MODES * W, W)
    other = to_core(mine)
    both = (2, MODES * W, W)
    object_grad, probe_grad = place_parts(
        gather_body, [(4, TILE, TILE), both], (*quarters, mine), "gather"
    )
    (probe_grad,) = place_parts(other_body, [both], (probe_grad, other), "other", {0: 0})
    return object_grad.reshape(specimen.shape), probe_grad.reshape(probe_modes.shape)


def solution(mesh):
    ny, ntx, nsc = mesh.devices.shape
    split = Mesh(mesh.devices.reshape(ny // 2, 2, ntx, nsc), ("x", "core", "tx", "scan"))
    rows = ("x", "core")
    placed = (
        P(None, None, rows, "tx"),
        P(),
        P(),
        P(rows, "tx", "scan", None),
        P(rows, "tx", "scan"),
        P(rows, "tx", "scan", None, None),
    )
    return jax.shard_map(
        functools.partial(per_device, (ny // 2, ntx, nsc)),
        mesh=split,
        in_specs=placed,
        out_specs=(P(None, None, rows, "tx"), P()),
        check_vma=False,
    )
```

```python
import functools

import jax
import jax.numpy as jnp
import numpy as np
from jax import lax
from jax.experimental import pallas as pl
from jax.experimental.pallas import tpu as pltpu
from jax.sharding import Mesh
from jax.sharding import PartitionSpec as P

F32 = jnp.float32
BF16 = jnp.bfloat16
VMEM = pl.BlockSpec(memory_space=pltpu.VMEM)
SMEM = pl.BlockSpec(memory_space=pltpu.SMEM)
ANY = pl.BlockSpec(memory_space=pl.ANY)
LONG = 10**10
CODE = 512
STEPS = (0, 2, 1, 3)
PARAMS = pltpu.CompilerParams(vmem_limit_bytes=48 * 1024 * 1024)
W = 128
HALF = 64
TILE = 256
MODES = 4


def call(body, outs, args, specs, scratch=(), name=None, flops=0):
    return pl.pallas_call(
        body,
        out_shape=[jax.ShapeDtypeStruct(shape, F32) for shape in outs],
        in_specs=specs,
        out_specs=[VMEM] * len(outs),
        scratch_shapes=list(scratch),
        compiler_params=PARAMS,
        cost_estimate=pl.CostEstimate(flops=flops, bytes_accessed=0, transcendentals=0) if flops else None,
        name=name,
    )(*args)


def copy_all(pairs, sems):
    copies = [
        pltpu.make_async_copy(source, target, sems.at[k])
        for k, (source, target) in enumerate(pairs)
    ]
    for copy in copies:
        copy.start()
    for copy in copies:
        copy.wait()


def low_lanes(rows):
    return lax.broadcasted_iota(jnp.int32, (rows, W), 1) < HALF


def swap(x):
    return pltpu.roll(x, HALF, 1)


def rim_rows(core, last):
    return pl.multiple_of((1 - core) * last, HALF), pl.multiple_of(core * last, HALF)


def fold_corner(rows, left, right):
    short = low_lanes(HALF // 2)
    upper, lower = rows[: HALF // 2], rows[HALF // 2 :]
    left[...] = jnp.where(short, upper[:, :W], swap(lower[:, :W]))
    right[...] = jnp.where(short, swap(upper[:, W:]), lower[:, W:])


def right_body(tile, to_right):
    wide = low_lanes(W)
    for part in range(4):
        first, second = tile[part, :W, W:], tile[part, W:, W:]
        to_right[part] = jnp.where(wide, swap(first), second)


def left_body(tile, after, to_left):
    wide = low_lanes(W)
    for part in range(4):
        first, second = tile[part, :W, :W], tile[part, W:, :W]
        to_left[part] = jnp.where(wide, first, swap(second))


def strips_body(tile, after, to_core, to_far, far_left, far_right):
    core_row, far_row = rim_rows(lax.axis_index("core"), TILE - HALF)
    for part in range(4):
        to_core[part] = tile[part, pl.ds(core_row, HALF), :]
        rows = tile[part, pl.ds(far_row, HALF), :]
        to_far[part] = rows
        fold_corner(rows, far_left.at[part], far_right.at[part])


def corners_body(from_right, from_left, out):
    core = lax.axis_index("core")
    low = low_lanes(HALF)
    span = pl.ds(pl.multiple_of((1 - core) * HALF, HALF), HALF)
    for part in range(4):
        right, left = from_right[part, span], from_left[part, span]
        right = jnp.where(core == 0, swap(right), right)
        left = jnp.where(core == 0, left, swap(left))
        out[part] = jnp.where(low, right, left)


def guard_body(far, right, left, mark):
    mark[...] = jnp.zeros_like(mark)


def phase_body(phase, real, imag):
    real[...] = jnp.cos(phase[...])
    imag[...] = jnp.sin(phase[...])


def halves(x):
    high = x.astype(BF16)
    return high, (x - high.astype(F32)).astype(BF16)


def times_right(real, imag, table):
    outs = ([], [])
    for k in range(0, len(real), 2):
        high, low = halves(
            jnp.concatenate(
                [jnp.concatenate([r, i], axis=1) for r, i in zip(real[k : k + 2], imag[k : k + 2])],
                axis=0,
            )
        )
        out = jnp.dot(jnp.concatenate([high, low, high], axis=1), table, preferred_element_type=F32)
        for m in range(2):
            outs[0].append(out[W * m : W * (m + 1), :W])
            outs[1].append(out[W * m : W * (m + 1), W:])
    return outs


def times_left(table, real, imag):
    outs = ([], [])
    for k in range(0, len(real), 2):
        high, low = halves(
            jnp.concatenate(
                [jnp.concatenate(real[k : k + 2], axis=1), jnp.concatenate(imag[k : k + 2], axis=1)],
                axis=0,
            )
        )
        out = jnp.dot(table, jnp.concatenate([high, low, high], axis=0), preferred_element_type=F32)
        for m in range(2):
            outs[0].append(out[:W, W * m : W * (m + 1)])
            outs[1].append(out[W:, W * m : W * (m + 1)])
    return outs


def slots_body(
    starts,
    live_counts,
    tile,
    from_right,
    from_left,
    from_core,
    from_far,
    far_right,
    far_left,
    corners,
    mark,
    probe,
    kernel_real,
    kernel_imag,
    measured,
    right_high,
    right_low,
    left_high,
    left_low,
    out0,
    out1,
    out2,
    out3,
    probe_send,
    probe_keep,
    wide,
    grads,
    probe_sum,
    mid,
    patches,
):
    core, scan = lax.axis_index("core"), lax.axis_index("scan")
    live = live_counts[0, 0, 0]
    core_row, far_row = rim_rows(core, TILE + HALF)
    tall = low_lanes(W)
    short = low_lanes(HALF // 2)
    for part in range(4):
        wide[part, 0, HALF : HALF + TILE] = tile[part, :, :W]
        wide[part, 1, HALF : HALF + TILE] = tile[part, :, W:]
        right, left = from_right[part], from_left[part]
        wide[part, 2, HALF : HALF + W] = jnp.where(tall, right, swap(left))
        wide[part, 2, HALF + W : HALF + TILE] = jnp.where(tall, swap(right), left)
        for row, strip in ((core_row, from_core), (far_row, from_far)):
            wide[part, 0, pl.ds(row, HALF)] = strip[part, :, :W]
            wide[part, 1, pl.ds(row, HALF)] = strip[part, :, W:]
        wide[part, 2, pl.ds(core_row, HALF)] = corners[part]
        right, left = far_right[part], far_left[part]
        wide[part, 2, pl.ds(far_row, HALF // 2)] = jnp.where(short, right, swap(left))
        lower = pl.multiple_of(far_row + HALF // 2, HALF // 2)
        wide[part, 2, pl.ds(lower, HALF // 2)] = jnp.where(short, swap(right), left)

    def corner(slot):
        return starts[2 * slot], starts[2 * slot + 1]

    forward_right = jnp.concatenate([right_high[...], right_high[...], right_low[...]], axis=0)
    inverse_right = jnp.concatenate([left_high[...], left_high[...], left_low[...]], axis=0)
    forward_left = jnp.concatenate([left_high[...], left_high[...], left_low[...]], axis=1)
    inverse_left = jnp.concatenate([right_high[...], right_high[...], right_low[...]], axis=1)

    def transform(real, imag):
        return times_left(forward_left, *times_right(real, imag, forward_right))

    def untransform(real, imag):
        return times_right(*times_left(inverse_left, real, imag), inverse_right)

    modes = range(MODES)
    lanes = lax.broadcasted_iota(jnp.int32, (W, W), 1)

    for slot in range(2):
        row, col = corner(slot)
        block = col // W
        shift = col - block * W
        after = jnp.where(block == 2, 0, block + 1)
        turn = jnp.where(shift == 0, 0, W - shift)
        for part in range(4):
            one = pltpu.roll(wide[part, block, pl.ds(row, W)], turn, 1)
            two = pltpu.roll(wide[part, after, pl.ds(row, W)], turn, 1)
            patches[4 * slot + part] = jnp.where(lanes < W - shift, one, two)
    slots = range(2)
    pairs = [(slot, m) for slot in slots for m in modes]

    def patch(part):
        return [patches[4 * slot + part] for slot in slots]

    def times(real, imag, by_real, by_imag):
        return (
            [r * by_real[s] - i * by_imag[s] for (s, m), r, i in zip(pairs, real, imag)],
            [r * by_imag[s] + i * by_real[s] for (s, m), r, i in zip(pairs, real, imag)],
        )

    def times_conj(real, imag, by_real, by_imag):
        return (
            [r * by_real[s] + i * by_imag[s] for (s, m), r, i in zip(pairs, real, imag)],
            [i * by_real[s] - r * by_imag[s] for (s, m), r, i in zip(pairs, real, imag)],
        )

    def total(terms):
        return [functools.reduce(jnp.add, terms[MODES * s : MODES * (s + 1)]) for s in slots]

    near_real, near_imag = patch(0), patch(1)
    real, imag = times(
        [probe[2 * m] for s, m in pairs], [probe[2 * m + 1] for s, m in pairs], near_real, near_imag
    )
    real, imag = transform(real, imag)
    kr, ki = [kernel_real[...]] * 2, [kernel_imag[...]] * 2
    real, imag = times(real, imag, kr, ki)
    real, imag = untransform(real, imag)
    for n in range(2 * MODES):
        mid[2 * n] = real[n]
        mid[2 * n + 1] = imag[n]
    away_real, away_imag = patch(2), patch(3)
    real, imag = times(real, imag, away_real, away_imag)
    real, imag = transform(real, imag)
    intensity = total([r * r + i * i for r, i in zip(real, imag)])
    residual = [
        (intensity[s] - measured[s]) * jnp.where(s < live, 2.0, 0.0).astype(F32) for s in slots
    ]
    real = [r * residual[s] for (s, m), r in zip(pairs, real)]
    imag = [i * residual[s] for (s, m), i in zip(pairs, imag)]
    real, imag = untransform(real, imag)
    both = range(2 * MODES)
    grad_real = total([mid[2 * n] * real[n] + mid[2 * n + 1] * imag[n] for n in both])
    grad_imag = total([mid[2 * n] * imag[n] - mid[2 * n + 1] * real[n] for n in both])
    for s in slots:
        grads[2, s] = grad_real[s]
        grads[3, s] = grad_imag[s]
    real, imag = times_conj(real, imag, patch(2), patch(3))
    real, imag = transform(real, imag)
    real, imag = times_conj(real, imag, kr, ki)
    real, imag = untransform(real, imag)
    grad_real = total([probe[2 * m] * real[n] + probe[2 * m + 1] * imag[n] for n, (s, m) in enumerate(pairs)])
    grad_imag = total([probe[2 * m] * imag[n] - probe[2 * m + 1] * real[n] for n, (s, m) in enumerate(pairs)])
    for s in slots:
        grads[0, s] = grad_real[s]
        grads[1, s] = grad_imag[s]
    real, imag = times_conj(real, imag, patch(0), patch(1))
    for m in modes:
        probe_sum[2 * m] = real[m] + real[MODES + m]
        probe_sum[2 * m + 1] = imag[m] + imag[MODES + m]

    places = lax.broadcasted_iota(jnp.int32, (8, W), 0)
    marks = jnp.zeros((8, W), F32)
    for slot in range(2):
        row, col = corner(slot)
        marks = jnp.where(places == slot, (row * CODE + col).astype(F32), marks)
    for step, out in enumerate((out0, out1, out2, out3)):
        part = lax.rem(scan + step, 4)
        for slot in range(2):
            out[W * slot : W * (slot + 1)] = grads[part, slot]
        out[2 * W :] = marks
    count = jnp.zeros((8, W), F32) + live.astype(F32)
    for half, out in ((core, probe_keep), (1 - core, probe_send)):
        for k in range(MODES):
            out[W * k : W * (k + 1)] = probe_sum[half * MODES + k]
        out[MODES * W :] = count


def spread_body(keep, got, out):
    rows = out.shape[1] - 8
    count = keep[MODES * W :] + got[MODES * W :]
    for k in range(out.shape[0]):
        span = slice(k * rows, (k + 1) * rows)
        out[k, :rows] = keep[span] + got[span]
        out[k, rows:] = count


def sum_body(chunks, after, out):
    out[...] = functools.reduce(jnp.add, [chunks[k] for k in range(chunks.shape[0])])


def pair_body(own, got, after, out):
    out[...] = own[...] + got[...]


def mean_body(own, got, spread):
    total = own[...] + got[...]
    rows = spread.shape[1]
    mean = total[:rows] / total[rows : rows + 1]
    for k in range(spread.shape[0]):
        spread[k] = mean


def by_parity(right, left):
    even = lax.rem(lax.axis_index("tx"), 2) == 0
    return jnp.where(even, right, left), jnp.where(even, left, right)


def place_body(one, two, three, four, first, second, wide):
    messages = (one, two, three, four)
    spots = []
    for message in messages:
        for slot in range(2):
            code = jnp.max(message[2 * W + slot : 2 * W + slot + 1]).astype(jnp.int32)
            row, col = code // CODE, lax.rem(code, CODE)
            row = jnp.clip(row, 0, TILE)
            col = jnp.clip(col, 0, 3 * W - 1)
            block = col // W
            after = jnp.where(block == 2, 0, block + 1)
            spots.append((row, block, after, col - block * W))
    wide[...] = jnp.zeros_like(wide)
    lanes = lax.broadcasted_iota(jnp.int32, (W, W), 1)
    for k, message in enumerate(messages):
        for slot in range(2):
            row, block, after, shift = spots[2 * k + slot]
            turned = pltpu.roll(message[W * slot : W * (slot + 1)], shift, 1)
            wide[block, pl.ds(row, W)] += jnp.where(lanes >= shift, turned, 0.0)
            wide[after, pl.ds(row, W)] += jnp.where(lanes < shift, turned, 0.0)
    half = (TILE + 2 * HALF) // 2
    low = low_lanes(half)
    upper, lower = wide[2, :half], wide[2, half:]
    right = jnp.where(low, upper, swap(lower))
    left = jnp.where(low, swap(upper), lower)
    first[...], second[...] = by_parity(right, left)


def rows_body(first, second, held, after, to_core, to_far, keep, wide):
    half = (TILE + 2 * HALF) // 2
    low = low_lanes(half)
    right, left = by_parity(first[...], second[...])
    wide[0, :half] = held[0, :half] + jnp.where(low, left, 0.0)
    wide[0, half:] = held[0, half:] + jnp.where(low, swap(left), 0.0)
    wide[1, :half] = held[1, :half] + jnp.where(low, 0.0, swap(right))
    wide[1, half:] = held[1, half:] + jnp.where(low, 0.0, right)
    core_row, far_row = rim_rows(lax.axis_index("core"), TILE + HALF)
    for k in range(2):
        to_core[k] = wide[k, pl.ds(core_row, HALF)]
        to_far[k] = wide[k, pl.ds(far_row, HALF)]
        keep[k] = wide[k, HALF : HALF + TILE]


def finish_body(from_core, from_far, held, after, out):
    core_row, far_row = rim_rows(lax.axis_index("core"), TILE - HALF)
    for k in range(2):
        span = slice(k * W, (k + 1) * W)
        out[:, span] = held[k]
        out[pl.ds(core_row, HALF), span] += from_core[k]
        out[pl.ds(far_row, HALF), span] += from_far[k]


def gather_body(one, two, three, four, mine, object_grad, probe_grad, sems):
    scan, core = lax.axis_index("scan"), lax.axis_index("core")
    parts = zip(STEPS, (one, two, three, four))
    pairs = [(part, object_grad.at[lax.rem(scan + 4 - step, 4)]) for step, part in parts]
    copy_all(pairs + [(mine, probe_grad.at[core])], sems)


def other_body(probe_grad, other, out, sems):
    copy_all([(other, out.at[1 - lax.axis_index("core")])], sems)


def place_parts(body, shapes, parts, name, aliases=None):
    return pl.pallas_call(
        body,
        out_shape=[jax.ShapeDtypeStruct(shape, F32) for shape in shapes],
        in_specs=[ANY] * len(parts),
        out_specs=[ANY] * len(shapes),
        scratch_shapes=[pltpu.SemaphoreType.DMA((len(parts),))],
        compiler_params=PARAMS,
        cost_estimate=pl.CostEstimate(flops=LONG, bytes_accessed=0, transcendentals=0),
        input_output_aliases=aliases or {},
        name=name,
    )(*parts)


def tables():
    index = np.arange(W)
    angle = 2.0 * np.pi * ((index[:, None] * index[None, :]) % W) / W
    cos, sin = np.cos(angle) / np.sqrt(W), -np.sin(angle) / np.sqrt(W)
    right = np.block([[cos, sin], [-sin, cos]])
    arrays = []
    for table in (right, right.T):
        high = table.astype(BF16)
        low = (table - high.astype(np.float64)).astype(BF16)
        arrays += [high, low]
    return [jnp.asarray(a) for a in arrays]


def run_slots(*args):
    message = (2 * W + 8, W)
    share = (MODES * W + 8, W)
    return call(
        slots_body,
        [message] * 4 + [share] * 2,
        (*args, *tables()),
        [SMEM] * 2 + [VMEM] * 8 + [ANY] + [VMEM] * 8,
        scratch=[
            pltpu.VMEM((4, 3, TILE + 2 * HALF, W), F32),
            pltpu.VMEM((4, 2, W, W), F32),
            pltpu.VMEM((2 * MODES, W, W), F32),
            pltpu.VMEM((4 * MODES, W, W), F32),
            pltpu.VMEM((8, W, W), F32),
        ],
        name="slots",
    )


def per_device(sizes, specimen, probe_modes, kernel_phase, offsets, live_counts, measured):
    nx, ntx, nsc = sizes

    def over_grid(target):
        pairs = []
        for x in range(nx):
            for c in range(2):
                for t in range(ntx):
                    x2, c2, t2 = target(x, c, t)
                    pairs.append(((x * 2 + c) * ntx + t, ((x2 % nx) * 2 + c2) * ntx + t2 % ntx))
        return lambda value: lax.ppermute(value, ("x", "core", "tx"), pairs)

    def across(x, c):
        return x + (1 if c else -1), 1 - c

    to_left = over_grid(lambda x, c, t: (x, c, t - 1))
    to_right = over_grid(lambda x, c, t: (x, c, t + 1))
    to_first = over_grid(lambda x, c, t: (x, c, t ^ 1))
    to_second = over_grid(lambda x, c, t: (x, c, t + 1 if t % 2 else t - 1))
    to_core = over_grid(lambda x, c, t: (x, 1 - c, t))
    to_far = over_grid(lambda x, c, t: (*across(x, c), t))
    far_left = over_grid(lambda x, c, t: (*across(x, c), t - 1))
    far_right = over_grid(lambda x, c, t: (*across(x, c), t + 1))

    def to_scan(value, step):
        return lax.ppermute(value, "scan", [(s, (s + step) % nsc) for s in range(nsc)])

    def to_pair(value, mask):
        return lax.ppermute(value, "tx", [(t, t ^ mask) for t in range(ntx)])

    tile = specimen.reshape(4, TILE, TILE)
    strip, corner, side = (4, HALF, TILE), (4, HALF // 2, W), (4, W, W)
    (right,) = call(right_body, [side], (tile,), [VMEM], name="right")
    (left,) = call(left_body, [side], (tile, right), [VMEM, ANY], name="left", flops=LONG)
    near, far, corner_left, corner_right = call(
        strips_body,
        [strip, strip, corner, corner],
        (tile, left),
        [VMEM, ANY],
        name="strips",
        flops=LONG,
    )
    from_right, from_left = to_left(left), to_right(right)
    from_core, from_far = to_core(near), to_far(far)
    corner_right, corner_left = far_left(corner_left), far_right(corner_right)
    (corners,) = call(
        corners_body, [(4, HALF, W)], (from_right, from_left), [VMEM] * 2, name="corners"
    )
    corners = to_core(corners)
    (mark,) = call(
        guard_body,
        [(8, W)],
        (from_far, corner_right, corner_left),
        [ANY] * 3,
        name="guard",
        flops=LONG,
    )
    kernel_real, kernel_imag = call(
        phase_body, [(W, W)] * 2, (kernel_phase,), [VMEM], name="phase"
    )
    rows = jnp.clip(offsets[0, 0, :, 0] + HALF, 0, TILE)
    cols = jnp.clip(offsets[0, 0, :, 1], -HALF, TILE - HALF)
    starts = jnp.stack([rows, jnp.where(cols < 0, cols + 3 * W, cols)], axis=1).reshape(4)
    outs = run_slots(
        starts,
        live_counts,
        tile,
        from_right,
        from_left,
        from_core,
        from_far,
        corner_right,
        corner_left,
        corners,
        mark,
        probe_modes.reshape(2 * MODES, W, W),
        kernel_real,
        kernel_imag,
        measured[0, 0],
    )
    own, away, probe_send, probe_keep = outs[0], outs[1:4], outs[4], outs[5]
    arrived = [to_scan(value, step) for step, value in enumerate(away, 1)]
    probe_got = to_core(probe_send)
    peers = nx * nsc
    rows = MODES * W // peers
    (chunks,) = call(
        spread_body,
        [(peers, rows + 8, W)],
        (probe_keep, probe_got),
        [VMEM] * 2,
        name="spread",
        flops=LONG,
    )
    chunks = lax.all_to_all(chunks, ("x", "scan"), 0, 0)
    tall = TILE + 2 * HALF
    first, second, held = call(
        place_body,
        [(tall // 2, W)] * 2 + [(3, tall, W)],
        (own, *arrived),
        [VMEM] * 4,
        name="place",
        flops=LONG,
    )
    (share,) = call(
        sum_body, [(rows + 8, W)], (chunks, first), [VMEM, ANY], name="sum", flops=LONG
    )
    first, second = to_first(first), to_second(second)
    got = to_pair(share, 1)
    near, far, held = call(
        rows_body,
        [(2, HALF, W)] * 2 + [(2, TILE, W)],
        (first, second, held, share),
        [VMEM] * 3 + [ANY],
        scratch=[pltpu.VMEM((2, tall, W), F32)],
        name="rows",
        flops=LONG,
    )
    (share,) = call(
        pair_body, [(rows + 8, W)], (share, got, near), [VMEM] * 2 + [ANY], name="pair", flops=LONG
    )
    got = to_pair(share, 2)
    near, far = to_core(near), to_far(far)
    (quarter,) = call(
        finish_body,
        [(TILE, TILE)],
        (near, far, held, share),
        [VMEM] * 3 + [ANY],
        name="finish",
        flops=LONG,
    )
    quarters = [quarter] + [to_scan(quarter, step) for step in STEPS[1:]]
    (share,) = call(
        pair_body, [(rows + 8, W)], (share, got, quarter), [VMEM] * 2 + [ANY], name="pair", flops=LONG
    )
    got = to_pair(share, ntx - 1)
    (spread,) = call(
        mean_body,
        [(peers, rows, W)],
        (share, got),
        [VMEM] * 2,
        name="mean",
        flops=LONG,
    )
    mine = lax.all_to_all(spread, ("x", "scan"), 0, 0).reshape(MODES * W, W)
    other = to_core(mine)
    both = (2, MODES * W, W)
    object_grad, probe_grad = place_parts(
        gather_body, [(4, TILE, TILE), both], (*quarters, mine), "gather"
    )
    (probe_grad,) = place_parts(other_body, [both], (probe_grad, other), "other", {0: 0})
    return object_grad.reshape(specimen.shape), probe_grad.reshape(probe_modes.shape)


def solution(mesh):
    ny, ntx, nsc = mesh.devices.shape
    split = Mesh(mesh.devices.reshape(ny // 2, 2, ntx, nsc), ("x", "core", "tx", "scan"))
    rows = ("x", "core")
    placed = (
        P(None, None, rows, "tx"),
        P(),
        P(),
        P(rows, "tx", "scan", None),
        P(rows, "tx", "scan"),
        P(rows, "tx", "scan", None, None),
    )
    return jax.shard_map(
        functools.partial(per_device, (ny // 2, ntx, nsc)),
        mesh=split,
        in_specs=placed,
        out_specs=(P(None, None, rows, "tx"), P()),
        check_vma=False,
    )
```
